128 devices in a mesh: user: 16 (over y, z), item: 8 (over x, core).
Axes of the slice: x: 4, y: 4, z: 4, core: 2. Of those that a mesh axis runs over, the one named last changes fastest.
Arguments:
- theta_shape: float32 [32768, 1024], P('user', 'item'), may hold values from 0.3 to 3
- theta_rate: float32 [32768, 1024], P('user', 'item'), may hold values from 100 to 1000
- xi_rate: float32 [32768], P('user'), may hold values from 1 to 10
- beta_shape: float32 [8192, 1024], P('item', 'user'), may hold values from 0.3 to 3
- beta_rate: float32 [8192, 1024], P('item', 'user'), may hold values from 50 to 500
- eta_rate: float32 [8192], P('item'), may hold values from 1 to 10
- tile_slots: int32 [16, 8, 32], P('user', 'item'), may hold values from 0 to 31, as said below
- tile_counts: bfloat16 [16, 8, 32, 256, 256], P('user', 'item'), may hold values from 0 to 5, as said below
- live_tiles: int32 [16, 8], P('user', 'item'), may hold values from 1 to 32, as said below
Outputs:
- theta_shape_new: float32 [32768, 1024], P('user', 'item')
- theta_log_rate: float32 [32768, 1024], P('user', 'item')
- xi_rate_new: float32 [32768], P('user')
- beta_shape_new: float32 [8192, 1024], P('item', 'user')
- beta_log_rate: float32 [8192, 1024], P('item', 'user')
- eta_rate_new: float32 [8192], P('item')
The draws below stay inside these ranges and needn't reach their ends.
Inputs may be any that keep to these rules, and one draw needn't show every extreme that they name: `tile_slots`: within one device's 32 slots the positions are distinct. `tile_counts`: whole numbers. `live_tiles`: some device uses all 32 slots.
All inputs are finite; a program needn't handle non-finite values.
Results may differ from the reference program's by a relative error of at most 0.0029.
Values may be sent and summed in bfloat16 or wider, within the bound.
A program may use at most 128 MiB of HBM per device.

```python
import math
import jax
import jax.numpy as jnp
from jax import lax

K = 1024
BLK = 256
UB = 8
IB = 4
TMAX = 32
NU = 32768
NI = 8192
N_USER = 16
N_ITEM = 8


def draw_tile_slots(key, part):
    device_keys = jax.random.split(key, N_USER * N_ITEM)
    orders = jax.vmap(lambda device_key: jax.random.permutation(device_key, UB * IB))(device_keys)
    return orders[:, :TMAX].reshape(N_USER, N_ITEM, TMAX).astype(jnp.int32)


def draw_tile_counts(key, part):
    values = jax.random.randint(key, (N_USER, N_ITEM, TMAX, BLK, BLK), 0, 6)
    return values.astype(jnp.float32).astype(jnp.bfloat16)


def draw_live_tiles(key, part):
    key_rank = jax.random.fold_in(key, 11)
    key_chosen = jax.random.fold_in(key, 23)
    ranked = jax.random.randint(key_rank, (N_USER * N_ITEM,), 1, TMAX + 1)
    loaded = jnp.maximum(1, ranked * ranked // TMAX)
    chosen = jax.random.randint(key_chosen, (), 0, N_USER * N_ITEM)
    loaded = jnp.where(jnp.arange(N_USER * N_ITEM) == chosen, TMAX, loaded)
    return loaded.reshape(N_USER, N_ITEM).astype(jnp.int32)


def block_levels(stream_key, extent, pieces, smallest, top_value):
    loudness, own = 1.0, jax.random.fold_in(stream_key, 6)
    for axis_at, shards_of in pieces:
        heights = jnp.exp(jax.random.uniform(jax.random.fold_in(own, axis_at), (shards_of,), jnp.float32, smallest / len(pieces), top_value / len(pieces)))
        loudness = loudness * jnp.repeat(heights, extent[axis_at] // shards_of).reshape([-1 if axis == axis_at else 1 for axis in range(len(extent))])
    return loudness


def setup_inputs(seed: int = 0) -> dict:
    keys = jax.random.split(jax.random.key(seed), 10)
    return {
        "theta_shape": jnp.clip(jnp.exp(math.log(3.0) - 2.3025851 * jax.random.uniform(keys[0], (NU, K), jnp.float32) ** block_levels(keys[0], (NU, K), ((0, 16), (1, 8)), -0.2, 0.2)), 0.3, 3.0),
        "theta_rate": jnp.clip(jnp.exp(math.log(1000.0) - 2.3025851 * jax.random.uniform(keys[1], (NU, K), jnp.float32) ** block_levels(keys[1], (NU, K), ((0, 16), (1, 8)), -0.2, 0.2)), 100.0, 1000.0),
        "xi_rate": jnp.clip(jnp.exp(math.log(10.0) - 2.3025851 * jax.random.uniform(keys[2], (NU,), jnp.float32) ** block_levels(keys[2], (NU,), ((0, 16),), -0.2, 0.2)), 1.0, 10.0),
        "beta_shape": jnp.clip(jnp.exp(math.log(3.0) - 2.3025851 * jax.random.uniform(keys[3], (NI, K), jnp.float32) ** block_levels(keys[3], (NI, K), ((0, 8), (1, 16)), -0.2, 0.2)), 0.3, 3.0),
        "beta_rate": jnp.clip(jnp.exp(math.log(500.0) - 2.3025851 * jax.random.uniform(keys[4], (NI, K), jnp.float32) ** block_levels(keys[4], (NI, K), ((0, 8), (1, 16)), -0.2, 0.2)), 50.0, 500.0),
        "eta_rate": jnp.clip(jnp.exp(math.log(10.0) - 2.3025851 * jax.random.uniform(keys[5], (NI,), jnp.float32) ** block_levels(keys[5], (NI,), ((0, 8),), -0.2, 0.2)), 1.0, 10.0),
        "tile_slots": draw_tile_slots(jax.random.fold_in(keys[9], 71), 0),
        "tile_counts": draw_tile_counts(jax.random.fold_in(keys[9], 71), 0),
        "live_tiles": draw_live_tiles(jax.random.fold_in(keys[9], 71), 0),
    }


prior_a = 0.3
prior_a2 = 0.3
prior_b2 = 1.0
prior_c = 0.3
prior_c2 = 0.3
prior_d2 = 1.0


def exp_mean_log(shape_param, rate_param):
    return jnp.exp(lax.digamma(shape_param) - jnp.log(rate_param)).astype(jnp.bfloat16)


def reference(theta_shape, theta_rate, xi_rate, beta_shape, beta_rate, eta_rate, tile_slots, tile_counts, live_tiles):
    theta_exp = exp_mean_log(theta_shape, theta_rate)
    beta_exp = exp_mean_log(beta_shape, beta_rate)

    def device_step(device, accum):
        row_shard = (device // N_ITEM).astype(jnp.int32)
        col_shard = (device % N_ITEM).astype(jnp.int32)
        slot_list = tile_slots[row_shard, col_shard]

        def tile_step(slot, inner):
            user_acc, item_acc = inner
            position = slot_list[slot]
            user_start = ((row_shard * UB + position // IB) * BLK).astype(jnp.int32)
            item_start = ((col_shard * IB + position % IB) * BLK).astype(jnp.int32)
            users = lax.dynamic_slice_in_dim(theta_exp, user_start, BLK, 0)
            items = lax.dynamic_slice_in_dim(beta_exp, item_start, BLK, 0)
            counts = tile_counts[row_shard, col_shard, slot].astype(jnp.float32)
            denominator = jnp.dot(users, items.T, preferred_element_type=jnp.float32)
            ratio_tile = (counts / denominator).astype(jnp.bfloat16)
            user_terms = jnp.dot(ratio_tile, items, preferred_element_type=jnp.float32)
            item_terms = jnp.dot(ratio_tile.T, users, preferred_element_type=jnp.float32)
            old_user = lax.dynamic_slice_in_dim(user_acc, user_start, BLK, 0)
            old_item = lax.dynamic_slice_in_dim(item_acc, item_start, BLK, 0)
            user_acc = lax.dynamic_update_slice_in_dim(user_acc, old_user + user_terms, user_start, 0)
            item_acc = lax.dynamic_update_slice_in_dim(item_acc, old_item + item_terms, item_start, 0)
            return (user_acc, item_acc)

        return lax.fori_loop(0, live_tiles[row_shard, col_shard], tile_step, accum)

    start_acc = (jnp.zeros((NU, K), jnp.float32), jnp.zeros((NI, K), jnp.float32))
    user_sum, item_sum = lax.fori_loop(0, N_USER * N_ITEM, device_step, start_acc)

    beta_total = jnp.sum(beta_shape / beta_rate, axis=0)
    theta_total = jnp.sum(theta_shape / theta_rate, axis=0)

    theta_shape_new = prior_a + theta_exp.astype(jnp.float32) * user_sum
    theta_rate_new = ((prior_a2 + K * prior_a) / xi_rate)[:, None] + beta_total[None, :]
    xi_rate_new = prior_a2 / prior_b2 + jnp.sum(theta_shape_new / theta_rate_new, axis=1)

    beta_shape_new = prior_c + beta_exp.astype(jnp.float32) * item_sum
    beta_rate_new = ((prior_c2 + K * prior_c) / eta_rate)[:, None] + theta_total[None, :]
    eta_rate_new = prior_c2 / prior_d2 + jnp.sum(beta_shape_new / beta_rate_new, axis=1)

    return (theta_shape_new, jnp.log(theta_rate_new), xi_rate_new, beta_shape_new, jnp.log(beta_rate_new), eta_rate_new)
```

```python
import jax
import jax.numpy as jnp
from jax import lax
from jax.experimental import pallas as pl
from jax.experimental.pallas import tpu as pltpu
from jax.sharding import PartitionSpec as P

prior_a = 0.3
prior_a2 = 0.3
prior_b2 = 1.0
prior_c = 0.3
prior_c2 = 0.3
prior_d2 = 1.0

K = 1024
UB = 8
BLK = 256
TMAX = 32
F32 = jnp.float32
BF16 = jnp.bfloat16
MESH = pl.DeviceIdType.MESH
SLOTS = 17
FIRST = 6


def exp_mean_log(s, r):
    w = s * (s + 3.0)
    prod = w * (w + 2.0)
    y = s + 4.0
    yr = y * r
    inv = 1.0 / (prod * yr)
    inv_prod = inv * yr
    v = inv * prod * r
    inv_r = inv * prod * y
    rec = (2.0 * s + 3.0) * (2.0 * w + 2.0) * inv_prod
    v2 = v * v
    series = v2 * (1.0 / 12 - v2 * (1.0 / 120 - v2 * (1.0 / 252 - v2 * (1.0 / 240))))
    return y * jnp.exp(-(rec + 0.5 * v + series)) * inv_r, s * inv_r


def kernel(
    slots_ref,
    live_ref,
    th_s,
    th_r,
    be_s,
    be_r,
    counts,
    xi_ref,
    eta_ref,
    out_user,
    out_item,
    out_xi,
    out_eta,
    out_tot,
    th_s_v,
    th_r_v,
    be_s_v,
    be_r_v,
    counts_v,
    TF,
    BT,
    R,
    IT,
    UF,
    U16,
    UR,
    S1s,
    S1r,
    S2s,
    S2r,
    J1s,
    J1r,
    J2s,
    J2r,
    J3s,
    J3r,
    ou_v,
    TL,
    TS0,
    TS1,
    TS2,
    TR1,
    TR2,
    TR3,
    TTc,
    XIP,
    XR,
    EP0,
    EP1,
    ER1,
    ER2,
    lsem,
    osem,
    gS,
    gR,
    bS,
    bR,
    sS,
    sR,
    s1S,
    s1R,
    s2S,
    s2R,
    jS,
    jR,
    tS,
    tR,
    eS,
    eR,
):
    user = lax.axis_index("user")
    item = lax.axis_index("item")
    x, c = item // 2, item % 2
    y, z = user // 4, user % 4
    q, p = item, user

    def m4(v):
        return (v + 4) % 4

    def dev(dx=0, dc=0, dy=0, dz=0):
        return (m4(y + dy) * 4 + m4(z + dz), m4(x + dx) * 2 + (c + dc) % 2)

    item_peers = [(dx, dc) for dx in range(4) for dc in range(2) if dx or dc]

    bar = pltpu.get_barrier_semaphore()
    for dx, dc in item_peers:
        pl.semaphore_signal(bar, inc=1, device_id=dev(dx=dx, dc=dc), device_id_type=MESH)
    for d in (1, 2, 3):
        pl.semaphore_signal(bar, inc=1, device_id=dev(dy=d), device_id_type=MESH)
        pl.semaphore_signal(bar, inc=1, device_id=dev(dz=d), device_id_type=MESH)

    def load(u, k):
        src, dst = ((th_s, th_s_v), (th_r, th_r_v))[k]
        return pltpu.make_async_copy(
            src.at[pl.ds(pl.multiple_of(u * BLK, BLK), BLK), :], dst.at[u], lsem.at[2 * u + k]
        )

    be_loads = [
        pltpu.make_async_copy(be_s, be_s_v, lsem.at[16]),
        pltpu.make_async_copy(be_r, be_r_v, lsem.at[17]),
    ]
    counts_load = pltpu.make_async_copy(counts, counts_v, lsem.at[18])
    for d in be_loads:
        d.start()
    for u in range(UB):
        load(u, 0).start()
        load(u, 1).start()
    counts_load.start()

    def rc(src, dst, ss, rs, to):
        return pltpu.make_async_remote_copy(
            src_ref=src, dst_ref=dst, send_sem=ss, recv_sem=rs, device_id=to, device_id_type=MESH
        )

    def total_item(k, n):
        dx, dc = item_peers[n]
        return rc(TS0.at[k], TR1.at[k, q], tS.at[k, n], tR.at[k, n], dev(dx=dx, dc=dc))

    def total_z(k, d):
        return rc(TS1.at[k], TR2.at[k, z], tS.at[k, 6 + d], tR.at[k, 6 + d], dev(dz=d))

    def total_y(k, d):
        return rc(TS2.at[k], TR3.at[k, y], tS.at[k, 9 + d], tR.at[k, 9 + d], dev(dy=d))

    def total_1(k):
        TR1[k, q] = TS0[k]
        for n in range(7):
            total_item(k, n).start()

    def total_2(k):
        for n in range(7):
            total_item(k, n).wait()
        TS1[k] = jnp.sum(TR1[k], axis=0)
        TR2[k, z] = TS1[k]
        for d in (1, 2, 3):
            total_z(k, d).start()

    def total_3(k):
        for d in (1, 2, 3):
            total_z(k, d).wait()
        TS2[k] = jnp.sum(TR2[k], axis=0)
        TR3[k, y] = TS2[k]
        for d in (1, 2, 3):
            total_y(k, d).start()

    def total_4(k):
        for d in (1, 2, 3):
            total_y(k, d).wait()
        out_tot[k] = jnp.sum(TR3[k], axis=0)

    A, B = slice(0, 32), slice(32, 64)

    def b1(h, ab, d):
        rows = (A, B)[ab]
        ref = BT.at[h, y, z, rows, :]
        return rc(ref, ref, bS.at[h, ab, d - 1], bR.at[h, ab, d - 1], dev(dy=d) if ab == 0 else dev(dz=d))

    def b2(h, ab, n):
        step = (1, 3)[n]
        if ab == 0:
            ref, to = BT.at[h, :, z, A, :], dev(dz=step)
        else:
            ref, to = BT.at[h, y, :, B, :], dev(dy=step)
        return rc(ref, ref, bS.at[h, ab, 3 + n], bR.at[h, ab, 3 + n], to)

    def b3(h, ab, n):
        step, back = ((1, 3), (3, 1))[n]
        two = slice(0, 2) if n == 0 else slice(2, 4)
        if ab == 0:
            ref, to = BT.at[h, two, m4(z + back), A, :], dev(dz=step)
        else:
            ref, to = BT.at[h, m4(y + back), two, B, :], dev(dy=step)
        return rc(ref, ref, bS.at[h, ab, 5 + n], bR.at[h, ab, 5 + n], to)

    def beta_2(h):
        for ab in range(2):
            for d in (1, 2, 3):
                b1(h, ab, d).wait_recv()
            for n in range(2):
                b2(h, ab, n).start()

    def beta_3(h):
        for ab in range(2):
            for n in range(2):
                b2(h, ab, n).wait_recv()
            for n in range(2):
                b3(h, ab, n).start()

    def beta_4(h):
        for ab in range(2):
            for n in range(2):
                b3(h, ab, n).wait_recv()

    def g(u, n):
        sems = dict(ss=gS.at[u, n], rs=gR.at[u, n])
        q1, q3, q2 = m4(x + 1) * 2 + c, m4(x + 3) * 2 + c, m4(x + 2) * 2 + c
        ref, to = {
            0: (lambda: (TF.at[q, u], dev(dx=1))),
            1: (lambda: (TF.at[q, u], dev(dx=3))),
            2: (lambda: (TF.at[q, u], dev(dc=1))),
            3: (lambda: (TF.at[q3, u, pl.ds(0, 128), :], dev(dx=1))),
            4: (lambda: (TF.at[q1, u, pl.ds(128, 128), :], dev(dx=3))),
            5: (lambda: (TF.at[q3, u], dev(dc=1))),
            6: (lambda: (TF.at[q1, u], dev(dc=1))),
            7: (lambda: (TF.at[q2, u], dev(dc=1))),
        }[n]()
        return rc(ref, ref, sems["ss"], sems["rs"], to)

    def own(u):
        load(u, 0).wait()
        load(u, 1).wait()
        e, mean = exp_mean_log(th_s_v[u], th_r_v[u])
        TF[q, u] = e.astype(BF16)
        TL[...] += jnp.sum(mean.reshape(32, 8, 128), axis=0)
        for n in (0, 1, 2):
            g(u, n).start()

    def forward_1(u):
        g(u, 0).wait_recv()
        g(u, 3).start()
        g(u, 5).start()
        g(u, 1).wait_recv()
        g(u, 4).start()
        g(u, 6).start()

    def forward_2(u):
        g(u, 3).wait_recv()
        g(u, 4).wait_recv()
        g(u, 7).start()

    def gathered(u):
        for n in (2, 5, 6, 7):
            g(u, n).wait_recv()

    def tiles(u):
        gathered(u)
        t_blocks = [
            jnp.concatenate([TF[2 * kb, u], TF[2 * kb + 1, u]], axis=1) for kb in range(4)
        ]
        t_all = jnp.concatenate(t_blocks, axis=1)
        live = live_ref[0]
        for j in range(4):
            h, n = j // 2, j % 2
            cols = slice(n * 256, (n + 1) * 256)
            weights = BT[h, :, :, :, cols].reshape(K, 256)
            denominator = jnp.dot(t_all, weights, preferred_element_type=F32)
            pos = u * 4 + j
            slot = jnp.int32(0)
            for t in range(TMAX):
                slot = jnp.where(slots_ref[t] == pos, t, slot)
            mask = (slot < live).astype(F32)
            tile_counts = counts_v[slot].astype(F32) * mask
            R[h, :, cols] = (tile_counts / denominator).astype(BF16)
        r_blocks = [R[0], R[1]]
        x_col = []
        for r in range(2):
            row = (prior_a2 + K * prior_a) / xi_ref[pl.ds(2 * u + r, 1), :]
            x_col.append(jnp.broadcast_to(row, (128, 128)).T)
        xi_mean = jnp.concatenate(x_col, axis=0)
        acc = jnp.zeros((256, 128), F32)
        for kb in range(4):
            terms = None
            for h in range(2):
                part = lax.dot_general(
                    r_blocks[h],
                    BT[h, kb].reshape(256, 512),
                    (((1,), (1,)), ((), ())),
                    preferred_element_type=F32,
                )
                terms = part if terms is None else terms + part
            for half in range(2):
                k8 = 2 * kb + half
                block = terms[:, half * 128 : (half + 1) * 128]
                UF[u, k8] = block
                U16[u, k8 // 2, k8 % 2] = block.astype(BF16)
                t = t_blocks[kb][:, half * 128 : (half + 1) * 128].astype(F32)
                rate = xi_mean + out_tot[0, k8 : k8 + 1, :]
                acc = acc + (prior_a / 8 + t * block) / rate
        rows = [jnp.sum(acc[r * 128 : (r + 1) * 128].T, axis=0, keepdims=True) for r in range(2)]
        XIP[u] = jnp.concatenate(rows, axis=0)
        sib(u).start()
        for kb in range(4):
            t_t = t_blocks[kb].T
            for h in range(2):
                part = jnp.dot(t_t, r_blocks[h], preferred_element_type=F32)
                IT[h, kb] += part.reshape(4, 64, 512)

    def sib(u):
        return rc(U16.at[u, :, 1 - c], UR.at[u], sS.at[u], sR.at[u], dev(dc=1))

    def s1(u, n):
        rows = pl.ds(n * 128, 128)
        return rc(S1s.at[u, rows, :], S1r.at[u, rows, :], s1S.at[u, n], s1R.at[u, n], dev(dx=(1, 3)[n]))

    def s2(u, n):
        return rc(S2s.at[u, n], S2r.at[u, n], s2S.at[u, n], s2R.at[u, n], dev(dx=(1, 3)[n]))

    def reduce_1(u):
        sib(u).wait_recv()
        x2 = m4(x + 2)
        S1s[u] = (UF[u, 2 * x2 + c] + UR[u, x2].astype(F32)).astype(BF16)
        s1(u, 0).start()
        s1(u, 1).start()

    def reduce_2(u):
        for n in range(2):
            s1(u, n).wait_recv()
            xn = m4(x + (1, 3)[n])
            total = UF[u, 2 * xn + c] + UR[u, xn].astype(F32)
            got = S1r[u, pl.ds(n * 128, 128), :].astype(F32)
            mine, plain = total[n * 128 : (n + 1) * 128], total[(1 - n) * 128 : (2 - n) * 128]
            S2s[u, n, pl.ds(n * 128, 128), :] = (mine + got).astype(BF16)
            S2s[u, n, pl.ds((1 - n) * 128, 128), :] = plain.astype(BF16)
            s2(u, n).start()

    def write_user(u):
        return pltpu.make_async_copy(
            ou_v.at[u], out_user.at[pl.ds(pl.multiple_of(u * BLK, BLK), BLK), :], osem.at[u]
        )

    def reduce_3(u):
        s2(u, 0).wait_recv()
        s2(u, 1).wait_recv()
        total = UF[u, q] + UR[u, x].astype(F32) + S2r[u, 0].astype(F32) + S2r[u, 1].astype(F32)
        ou_v[u] = prior_a + TF[q, u].astype(F32) * total
        write_user(u).start()

    def blocks(ab, at):
        return (lambda h: IT[h, :, at, A, :]) if ab == 0 else (lambda h: IT[h, at, :, B, :])

    def along(ab, first):
        on_z = (ab == 0) == first
        return (z, lambda d: dev(dz=d)) if on_z else (y, lambda d: dev(dy=d))

    def j1(h, ab, n):
        _, to = along(ab, True)
        ref = pl.ds(2 * n, 2)
        return rc(J1s.at[h, ab, ref], J1r.at[h, ab, ref], jS.at[h, ab, n], jR.at[h, ab, n], to((1, 3)[n]))

    def j2(h, ab, n):
        _, to = along(ab, True)
        return rc(J2s.at[h, ab, n], J2r.at[h, ab, n], jS.at[h, ab, 2 + n], jR.at[h, ab, 2 + n], to((1, 3)[n]))

    def j3(h, ab, d):
        me, to = along(ab, False)
        return rc(
            J3s.at[h, ab, m4(me + d)], J3r.at[h, ab, d - 1], jS.at[h, ab, 3 + d], jR.at[h, ab, 3 + d], to(d)
        )

    def item_1(h):
        for ab in range(2):
            me, _ = along(ab, True)
            J1s[h, ab] = blocks(ab, m4(me + 2))(h).astype(BF16)
            for n in range(2):
                j1(h, ab, n).start()

    def item_2(h):
        for ab in range(2):
            me, _ = along(ab, True)
            for n in range(2):
                j1(h, ab, n).wait_recv()
                part = blocks(ab, m4(me + (1, 3)[n]))(h)
                two, rest = slice(2 * n, 2 * n + 2), slice(2 - 2 * n, 4 - 2 * n)
                J2s[h, ab, n, two] = (part[two] + J1r[h, ab, two].astype(F32)).astype(BF16)
                J2s[h, ab, n, rest] = part[rest].astype(BF16)
                j2(h, ab, n).start()

    def item_3(h):
        for ab in range(2):
            me, _ = along(ab, True)
            for n in range(2):
                j2(h, ab, n).wait_recv()
            total = blocks(ab, me)(h) + J2r[h, ab, 0].astype(F32) + J2r[h, ab, 1].astype(F32)
            J3s[h, ab] = total.astype(BF16)
            if ab == 0:
                IT[h, :, z, A, :] = total
            else:
                IT[h, y, :, B, :] = total
            for d in (1, 2, 3):
                j3(h, ab, d).start()

    def item_4(h):
        for ab in range(2):
            rows = (A, B)[ab]
            for d in (1, 2, 3):
                j3(h, ab, d).wait_recv()
            total = IT[h, y, z, rows, :] + jnp.sum(J3r[h, ab].astype(F32), axis=0)
            out_item[rows, h * 512 : (h + 1) * 512] = (
                prior_c + BT[h, y, z, rows, :].astype(F32) * total
            )

    def xi_send(n):
        dx, dc = item_peers[n]
        return rc(XIP, XR.at[q], eS.at[n], eR.at[n], dev(dx=dx, dc=dc))

    def xi_1():
        XR[q] = XIP[...]
        for n in range(7):
            xi_send(n).start()

    def xi_2():
        for n in range(7):
            xi_send(n).wait()
        out_xi[...] = prior_a2 / prior_b2 + jnp.sum(XR[...], axis=0)

    def eta_z(d):
        return rc(EP0, ER1.at[z], eS.at[6 + d], eR.at[6 + d], dev(dz=d))

    def eta_y(d):
        return rc(EP1, ER2.at[y], eS.at[9 + d], eR.at[9 + d], dev(dy=d))

    def eta_1():
        for k8 in range(8):
            row = out_tot[1, k8 : k8 + 1, :]
            TTc[k8] = jnp.broadcast_to(row, (128, 128)).T
        for h in range(2):
            em = jnp.concatenate(
                [(prior_c2 + K * prior_c) / eta_ref[h * 4 + r : h * 4 + r + 1, :] for r in range(4)], axis=1
            )

            def step(k16, acc):
                yy, zz = k16 // 4, k16 % 4
                tt = TTc[k16 // 2, pl.ds(pl.multiple_of((k16 % 2) * 64, 64), 64), :]
                rate = jnp.concatenate([tt] * 4, axis=1) + em
                val = (prior_c / 16 + BT[h, yy, zz].astype(F32) * IT[h, yy, zz]) / rate
                return acc + jnp.sum(val.reshape(8, 8, 512), axis=0)

            acc = lax.fori_loop(0, 16, step, jnp.zeros((8, 512), F32))
            EP0[h] = jnp.sum(acc, axis=0, keepdims=True)
        ER1[z] = EP0[...]
        for d in (1, 2, 3):
            eta_z(d).start()

    def eta_2():
        for d in (1, 2, 3):
            eta_z(d).wait()
        EP1[...] = jnp.sum(ER1[...], axis=0)
        ER2[y] = EP1[...]
        for d in (1, 2, 3):
            eta_y(d).start()

    def eta_3():
        for d in (1, 2, 3):
            eta_y(d).wait()
        out_eta[...] = prior_c2 / prior_d2 + jnp.sum(ER2[...], axis=0)

    for d in be_loads:
        d.wait()
    sums = jnp.zeros((64, 128), F32)
    for ib in range(8):
        rows = slice(ib * 128, (ib + 1) * 128)
        e, mean = exp_mean_log(be_s_v[rows, :].T, be_r_v[rows, :].T)
        BT[ib // 4, y, z, :, (ib % 4) * 128 : (ib % 4 + 1) * 128] = e.astype(BF16)
        sums = sums + mean
    row = jnp.sum(jnp.concatenate([sums, sums], axis=0).T, axis=0, keepdims=True)
    lane = lax.broadcasted_iota(jnp.int32, (8, 128), 1)
    sub = lax.broadcasted_iota(jnp.int32, (8, 128), 0)
    TS0[0] = jnp.where((sub == p // 2) & (lane // 64 == p % 2), jnp.broadcast_to(row, (8, 128)), 0.0)
    TL[...] = jnp.zeros_like(TL)
    pl.semaphore_wait(bar, 13)
    for h in range(2):
        for ab in range(2):
            for d in (1, 2, 3):
                b1(h, ab, d).start()
    total_1(0)
    IT[...] = jnp.zeros_like(IT)

    def slot_step(s, carry):
        def at(first, task):
            @pl.when((s >= first) & (s < first + UB))
            def _():
                task(s - first)

        def once(when, *tasks):
            @pl.when(s == when)
            def _():
                for task in tasks:
                    task()

        at(0, own)
        at(2, forward_1)
        at(3, forward_2)
        once(0, lambda: beta_2(0))
        once(1, lambda: beta_2(1), lambda: total_2(0))
        once(2, lambda: beta_3(0))
        once(3, lambda: beta_3(1), lambda: total_3(0))
        once(5, lambda: total_4(0), counts_load.wait)
        once(FIRST, lambda: beta_4(0), lambda: beta_4(1))
        at(FIRST, tiles)
        once(8, theta_total_1)
        once(9, lambda: total_2(1))
        once(10, lambda: total_3(1))
        once(11, lambda: total_4(1))
        once(FIRST + 7, lambda: item_1(0), lambda: item_1(1), xi_1)
        at(FIRST + 1, reduce_1)
        at(FIRST + 2, reduce_2)
        at(FIRST + 3, reduce_3)
        once(FIRST + 8, lambda: item_2(0), lambda: item_2(1), eta_1, xi_2)
        once(FIRST + 9, lambda: item_3(0), lambda: item_3(1), eta_2)
        once(FIRST + 10, lambda: item_4(0), lambda: item_4(1), eta_3)
        return carry

    def theta_total_1():
        local = jnp.sum(TL[...], axis=0, keepdims=True)
        TS0[1] = jnp.where(sub == q, jnp.broadcast_to(local, (8, 128)), 0.0)
        total_1(1)

    lax.fori_loop(0, SLOTS, slot_step, 0)

    def drain(u, carry):
        for n in range(8):
            g(u, n).wait_send()
        sib(u).wait_send()
        for n in range(2):
            s1(u, n).wait_send()
            s2(u, n).wait_send()
        write_user(u).wait()
        return carry

    lax.fori_loop(0, UB, drain, 0)
    for h in range(2):
        for ab in range(2):
            for d in (1, 2, 3):
                b1(h, ab, d).wait_send()
                j3(h, ab, d).wait_send()
            for n in range(2):
                b2(h, ab, n).wait_send()
                b3(h, ab, n).wait_send()
                j1(h, ab, n).wait_send()
                j2(h, ab, n).wait_send()


def on_device(theta_shape, theta_rate, xi_rate, beta_shape, beta_rate, eta_rate, tile_slots, tile_counts, live_tiles):
    user = lax.axis_index("user")
    item = lax.axis_index("item")
    smem = pl.BlockSpec(memory_space=pltpu.SMEM)
    vmem = pl.BlockSpec(memory_space=pltpu.VMEM)
    hbm = pl.BlockSpec(memory_space=pltpu.HBM)
    dma = pltpu.SemaphoreType.DMA
    V = pltpu.VMEM
    user_new, item_new, xi_new, eta_new, totals = pl.pallas_call(
        kernel,
        out_shape=(
            jax.ShapeDtypeStruct((2048, 128), F32),
            jax.ShapeDtypeStruct((64, 1024), F32),
            jax.ShapeDtypeStruct((8, 2, 128), F32),
            jax.ShapeDtypeStruct((2, 1, 512), F32),
            jax.ShapeDtypeStruct((2, 8, 128), F32),
        ),
        in_specs=[smem, smem, hbm, hbm, hbm, hbm, hbm, vmem, vmem],
        out_specs=(hbm, vmem, vmem, vmem, vmem),
        scratch_shapes=[
            V((8, 256, 128), F32),
            V((8, 256, 128), F32),
            V((1024, 64), F32),
            V((1024, 64), F32),
            V((32, 256, 256), BF16),
            V((8, 8, 256, 128), BF16),
            V((2, 4, 4, 64, 512), BF16),
            V((2, 256, 512), BF16),
            V((2, 4, 4, 64, 512), F32),
            V((8, 8, 256, 128), F32),
            V((8, 4, 2, 256, 128), BF16),
            V((8, 4, 256, 128), BF16),
            V((8, 256, 128), BF16),
            V((8, 256, 128), BF16),
            V((8, 2, 256, 128), BF16),
            V((8, 2, 256, 128), BF16),
            V((2, 2, 4, 32, 512), BF16),
            V((2, 2, 4, 32, 512), BF16),
            V((2, 2, 2, 4, 32, 512), BF16),
            V((2, 2, 2, 4, 32, 512), BF16),
            V((2, 2, 4, 32, 512), BF16),
            V((2, 2, 3, 32, 512), BF16),
            V((8, 256, 128), F32),
            V((8, 128), F32),
            V((2, 8, 128), F32),
            V((2, 8, 128), F32),
            V((2, 8, 128), F32),
            V((2, 8, 8, 128), F32),
            V((2, 4, 8, 128), F32),
            V((2, 4, 8, 128), F32),
            V((8, 128, 128), F32),
            V((8, 2, 128), F32),
            V((8, 8, 2, 128), F32),
            V((2, 1, 512), F32),
            V((2, 1, 512), F32),
            V((4, 2, 1, 512), F32),
            V((4, 2, 1, 512), F32),
            dma((19,)),
            dma((8,)),
            dma((8, 8)),
            dma((8, 8)),
            dma((2, 2, 7)),
            dma((2, 2, 7)),
            dma((8,)),
            dma((8,)),
            dma((8, 2)),
            dma((8, 2)),
            dma((8, 2)),
            dma((8, 2)),
            dma((2, 2, 7)),
            dma((2, 2, 7)),
            dma((2, 13)),
            dma((2, 13)),
            dma((13,)),
            dma((13,)),
        ],
        compiler_params=pltpu.CompilerParams(
            collective_id=0, has_side_effects=True, vmem_limit_bytes=58 * 2**20
        ),
        cost_estimate=pl.CostEstimate(flops=13 * 10**9, bytes_accessed=10 * 2**20, transcendentals=10**6),
        name="update",
    )(
        tile_slots.reshape(TMAX),
        live_tiles.reshape(1),
        theta_shape,
        theta_rate,
        beta_shape,
        beta_rate,
        tile_counts.reshape(TMAX, BLK, BLK),
        xi_rate.reshape(16, 128),
        eta_rate.reshape(8, 128),
    )
    beta_total, theta_total = totals[0].reshape(K), totals[1].reshape(K)
    beta_slice = lax.dynamic_slice_in_dim(beta_total, item * 128, 128, 0)
    theta_slice = lax.dynamic_slice_in_dim(theta_total, user * 64, 64, 0)
    xi_mean = (prior_a2 + K * prior_a) / xi_rate
    eta_mean = (prior_c2 + K * prior_c) / eta_rate
    return (
        user_new,
        jnp.log(xi_mean[:, None] + beta_slice[None, :]),
        xi_new.reshape(2048),
        item_new.T,
        jnp.log(eta_mean[:, None] + theta_slice[None, :]),
        eta_new.reshape(1024),
    )


def solution(mesh):
    in_specs = (
        P("user", "item"),
        P("user", "item"),
        P("user"),
        P("item", "user"),
        P("item", "user"),
        P("item"),
        P("user", "item", None),
        P("user", "item", None, None, None),
        P("user", "item"),
    )
    out_specs = (
        P("user", "item"),
        P("user", "item"),
        P("user"),
        P("item", "user"),
        P("item", "user"),
        P("item"),
    )
    return jax.shard_map(on_device, mesh=mesh, in_specs=in_specs, out_specs=out_specs, check_vma=False)
```

```python
import jax
import jax.numpy as jnp
from jax import lax
from jax.experimental import pallas as pl
from jax.experimental.pallas import tpu as pltpu
from jax.sharding import PartitionSpec as P

prior_a = 0.3
prior_a2 = 0.3
prior_b2 = 1.0
prior_c = 0.3
prior_c2 = 0.3
prior_d2 = 1.0

K = 1024
UB = 8
BLK = 256
TMAX = 32
F32 = jnp.float32
BF16 = jnp.bfloat16
MESH = pl.DeviceIdType.MESH
OWN = [0, 1, 2, 3, 4, 5, 6, 7]
FORWARD_1 = [4, 5, 6, 7, 9, 10, 11, 12]
FORWARD_2 = [7, 9, 11, 12, 13, 14, 15, 16]
TILES = [13, 15, 17, 18]
FIRST_HALF = [19, 20, 21, 22]
SECOND_HALF = [23, 24, 25, 26]
REDUCE_1 = [16, 17, 18, 19, 25, 26, 27, 28]
REDUCE_2 = [18, 19, 21, 22, 28, 29, 30, 31]
REDUCE_3 = [21, 22, 24, 26, 31, 32, 33, 34]
BETA_2 = [4, 5]
BETA_3 = [8, 10]
BETA_4 = [13, 13]
ITEM_1 = [22, 26]
ITEM_2 = [26, 29]
ITEM_3 = [30, 32]
ITEM_4 = [33, 35]
ETA = [27, 32, 35]
XI = [26, 31]
TOTAL_BETA = [6, 8, 10]
TOTAL_THETA = [9, 13, 16, 19]
CLEAR = 3
SLOTS = 36


def exp_mean_log(s, r):
    w = s * (s + 3.0)
    prod = w * (w + 2.0)
    y = s + 4.0
    yr = y * r
    inv = 1.0 / (prod * yr)
    inv_prod = inv * yr
    v = inv * prod * r
    inv_r = inv * prod * y
    rec = (2.0 * s + 3.0) * (2.0 * w + 2.0) * inv_prod
    v2 = v * v
    series = v2 * (1.0 / 12 - v2 * (1.0 / 120 - v2 * (1.0 / 252 - v2 * (1.0 / 240))))
    return y * jnp.exp(-(rec + 0.5 * v + series)) * inv_r, s * inv_r


def kernel(
    slots_ref,
    live_ref,
    th_s,
    th_r,
    be_s,
    be_r,
    counts,
    xi_ref,
    eta_ref,
    out_user,
    out_item,
    out_xi,
    out_eta,
    out_tot,
    th_s_v,
    th_r_v,
    be_s_v,
    be_r_v,
    counts_v,
    TF,
    BT,
    R,
    IT,
    UF,
    U16,
    UR,
    S1s,
    S1r,
    S2s,
    S2r,
    J1s,
    J1r,
    J2s,
    J2r,
    J3s,
    J3r,
    TL,
    TS0,
    TS1,
    TS2,
    TR1,
    TR2,
    TR3,
    TTc,
    XIP,
    XR,
    EP0,
    EP1,
    ER1,
    ER2,
    lsem,
    gR,
    rR,
    jR,
    tR,
    send,
):
    user = lax.axis_index("user")
    item = lax.axis_index("item")
    x, c = item // 2, item % 2
    y, z = user // 4, user % 4
    q, p = item, user

    def m4(v):
        return (v + 4) % 4

    def dev(dx=0, dc=0, dy=0, dz=0):
        return (m4(y + dy) * 4 + m4(z + dz), m4(x + dx) * 2 + (c + dc) % 2)

    item_peers = [(dx, dc) for dx in range(4) for dc in range(2) if dx or dc]

    bar = pltpu.get_barrier_semaphore()
    for dx, dc in item_peers:
        pl.semaphore_signal(bar, inc=1, device_id=dev(dx=dx, dc=dc), device_id_type=MESH)
    for d in (1, 2, 3):
        pl.semaphore_signal(bar, inc=1, device_id=dev(dy=d), device_id_type=MESH)
        pl.semaphore_signal(bar, inc=1, device_id=dev(dz=d), device_id_type=MESH)

    be_loads = [
        pltpu.make_async_copy(be_s, be_s_v, lsem.at[0]),
        pltpu.make_async_copy(be_r, be_r_v, lsem.at[0]),
    ]
    first, later = pl.ds(0, BLK), pl.ds(BLK, 7 * BLK)
    th_loads = [
        pltpu.make_async_copy(th_s.at[first, :], th_s_v.at[first, :], lsem.at[1]),
        pltpu.make_async_copy(th_r.at[first, :], th_r_v.at[first, :], lsem.at[1]),
        pltpu.make_async_copy(th_s.at[later, :], th_s_v.at[later, :], lsem.at[2]),
        pltpu.make_async_copy(th_r.at[later, :], th_r_v.at[later, :], lsem.at[2]),
    ]
    counts_load = pltpu.make_async_copy(counts, counts_v, lsem.at[3])
    for d in be_loads + th_loads + [counts_load]:
        d.start()

    def landed(ref, sem):
        pltpu.make_async_copy(ref, ref, sem).wait()

    def rc(src, dst, ss, rs, to):
        return pltpu.make_async_remote_copy(
            src_ref=src, dst_ref=dst, send_sem=ss, recv_sem=rs, device_id=to, device_id_type=MESH
        )

    def total_item(k, n):
        dx, dc = item_peers[n]
        return rc(TS0.at[k], TR1.at[k, q], send.at[10], tR.at[3 * k], dev(dx=dx, dc=dc))

    def total_z(k, d):
        return rc(TS1.at[k], TR2.at[k, z], send.at[11], tR.at[3 * k + 1], dev(dz=d))

    def total_y(k, d):
        return rc(TS2.at[k], TR3.at[k, y], send.at[12], tR.at[3 * k + 2], dev(dy=d))

    def total_1(k):
        TR1[k, q] = TS0[k]
        for n in range(7):
            total_item(k, n).start()

    def total_2(k):
        landed(TR1.at[k, pl.ds(0, 7)], tR.at[3 * k])
        TS1[k] = jnp.sum(TR1[k], axis=0)
        TR2[k, z] = TS1[k]
        for d in (1, 2, 3):
            total_z(k, d).start()

    def total_3(k):
        landed(TR2.at[k, pl.ds(0, 3)], tR.at[3 * k + 1])
        TS2[k] = jnp.sum(TR2[k], axis=0)
        TR3[k, y] = TS2[k]
        for d in (1, 2, 3):
            total_y(k, d).start()

    def total_4(k):
        landed(TR3.at[k, pl.ds(0, 3)], tR.at[3 * k + 2])
        out_tot[k] = jnp.sum(TR3[k], axis=0)

    A, B = slice(0, 32), slice(32, 64)

    def b1(h, ab, d):
        rows = (A, B)[ab]
        ref = BT.at[h, y, z, rows, :]
        return rc(ref, ref, send.at[0], jR.at[0, h], dev(dy=d) if ab == 0 else dev(dz=d))

    def b2(h, ab, n):
        step = (1, 3)[n]
        if ab == 0:
            ref, to = BT.at[h, :, z, A, :], dev(dz=step)
        else:
            ref, to = BT.at[h, y, :, B, :], dev(dy=step)
        return rc(ref, ref, send.at[1], jR.at[1, h], to)

    def b3(h, ab, n):
        step, back = ((1, 3), (3, 1))[n]
        two = slice(0, 2) if n == 0 else slice(2, 4)
        if ab == 0:
            ref, to = BT.at[h, two, m4(z + back), A, :], dev(dz=step)
        else:
            ref, to = BT.at[h, m4(y + back), two, B, :], dev(dy=step)
        return rc(ref, ref, send.at[2], jR.at[2, h], to)

    def beta_2(h):
        landed(BT.at[h, pl.ds(0, 3), pl.ds(0, 2), A, :], jR.at[0, h])
        for ab in range(2):
            for n in range(2):
                b2(h, ab, n).start()

    def beta_3(h):
        landed(BT.at[h, pl.ds(0, 2)], jR.at[1, h])
        for ab in range(2):
            for n in range(2):
                b3(h, ab, n).start()

    def beta_4(h):
        landed(BT.at[h, 0], jR.at[2, h])

    def g(u, n):
        group = (0, 0, 2, 1, 1, 2, 2, 2)[n]
        q1, q3, q2 = m4(x + 1) * 2 + c, m4(x + 3) * 2 + c, m4(x + 2) * 2 + c
        ref, to = {
            0: (lambda: (TF.at[q, u], dev(dx=1))),
            1: (lambda: (TF.at[q, u], dev(dx=3))),
            2: (lambda: (TF.at[q, u], dev(dc=1))),
            3: (lambda: (TF.at[q3, u, pl.ds(0, 128), :], dev(dx=1))),
            4: (lambda: (TF.at[q1, u, pl.ds(128, 128), :], dev(dx=3))),
            5: (lambda: (TF.at[q3, u], dev(dc=1))),
            6: (lambda: (TF.at[q1, u], dev(dc=1))),
            7: (lambda: (TF.at[q2, u], dev(dc=1))),
        }[n]()
        return rc(ref, ref, send.at[3], gR.at[group, u], to)

    def own(u):
        @pl.when(u == 1)
        def _():
            th_loads[2].wait()
            th_loads[3].wait()

        rows = pl.ds(pl.multiple_of(u * BLK, BLK), BLK)
        e, mean = exp_mean_log(th_s_v[rows, :], th_r_v[rows, :])
        TF[q, u] = e.astype(BF16)
        TL[...] += jnp.sum(mean.reshape(32, 8, 128), axis=0)
        for n in (0, 1, 2):
            g(u, n).start()

    def forward_1(u):
        landed(TF.at[pl.ds(0, 2), u], gR.at[0, u])
        for n in (3, 5, 4, 6):
            g(u, n).start()

    def forward_2(u):
        landed(TF.at[0, u], gR.at[1, u])
        g(u, 7).start()

    def gathered(u):
        landed(TF.at[pl.ds(0, 4), u], gR.at[2, u])

    def user_block(u):
        return [jnp.concatenate([TF[2 * kb, u], TF[2 * kb + 1, u]], axis=1) for kb in range(4)]

    def ratios(u, h, t_all):
        live = live_ref[0, 0]
        for n in range(2):
            cols = slice(n * 256, (n + 1) * 256)
            weights = BT[h, :, :, :, cols].reshape(K, 256)
            denominator = jnp.dot(t_all, weights, preferred_element_type=F32)
            pos = u * 4 + h * 2 + n
            slot = jnp.int32(0)
            for t in range(TMAX):
                slot = jnp.where(slots_ref[t] == pos, t, slot)
            mask = (slot < live).astype(F32)
            tile_counts = counts_v[slot].astype(F32) * mask
            R[h, :, cols] = (tile_counts / denominator).astype(BF16)

    def user_terms(h, kb):
        return lax.dot_general(
            R[h], BT[h, kb].reshape(256, 512), (((1,), (1,)), ((), ())), preferred_element_type=F32
        )

    def item_terms(t_blocks, halves):
        for kb in range(4):
            t_t = t_blocks[kb].T
            for h in halves:
                part = jnp.dot(t_t, R[h], preferred_element_type=F32)
                IT[h, kb] += part.reshape(4, 64, 512)

    def finish(u, t_blocks, product):
        x_col = []
        for r in range(2):
            row = (prior_a2 + K * prior_a) / xi_ref[pl.ds(2 * u + r, 1), :]
            x_col.append(jnp.broadcast_to(row, (128, 128)).T)
        xi_mean = jnp.concatenate(x_col, axis=0)
        acc = jnp.zeros((256, 128), F32)
        for kb in range(4):
            terms = product(kb)
            for half in range(2):
                k8 = 2 * kb + half
                block = terms[half]
                UF[u, k8] = block
                U16[u, k8 // 2, k8 % 2] = block.astype(BF16)
                t = t_blocks[kb][:, half * 128 : (half + 1) * 128].astype(F32)
                rate = xi_mean + out_tot[0, k8 : k8 + 1, :]
                acc = acc + (prior_a / 8 + t * block) / rate
        rows = [jnp.sum(acc[r * 128 : (r + 1) * 128].T, axis=0, keepdims=True) for r in range(2)]
        XIP[u] = jnp.concatenate(rows, axis=0)
        sib(u).start()

    def tiles(u):
        gathered(u)
        t_blocks = user_block(u)
        t_all = jnp.concatenate(t_blocks, axis=1)
        ratios(u, 0, t_all)
        ratios(u, 1, t_all)

        def product(kb):
            terms = user_terms(0, kb) + user_terms(1, kb)
            return terms[:, :128], terms[:, 128:]

        finish(u, t_blocks, product)
        item_terms(t_blocks, (0, 1))

    def tiles_first(u):
        gathered(u)
        t_blocks = user_block(u)
        ratios(u, 0, jnp.concatenate(t_blocks, axis=1))
        for kb in range(4):
            terms = user_terms(0, kb)
            UF[u, 2 * kb] = terms[:, :128]
            UF[u, 2 * kb + 1] = terms[:, 128:]
        item_terms(t_blocks, (0,))

    def tiles_second(u):
        t_blocks = user_block(u)
        ratios(u, 1, jnp.concatenate(t_blocks, axis=1))

        def product(kb):
            terms = user_terms(1, kb)
            return UF[u, 2 * kb] + terms[:, :128], UF[u, 2 * kb + 1] + terms[:, 128:]

        finish(u, t_blocks, product)
        item_terms(t_blocks, (1,))

    def sib(u):
        return rc(U16.at[u, :, 1 - c], UR.at[u], send.at[4], rR.at[0, u], dev(dc=1))

    def s1(u, n):
        rows = pl.ds(n * 128, 128)
        return rc(S1s.at[u, rows, :], S1r.at[u, rows, :], send.at[5], rR.at[1, u], dev(dx=(1, 3)[n]))

    def s2(u, n):
        return rc(S2s.at[u, n], S2r.at[u, n], send.at[6], rR.at[2, u], dev(dx=(1, 3)[n]))

    def reduce_1(u):
        landed(UR.at[u], rR.at[0, u])
        x2 = m4(x + 2)
        S1s[u] = (UF[u, 2 * x2 + c] + UR[u, x2].astype(F32)).astype(BF16)
        s1(u, 0).start()
        s1(u, 1).start()

    def reduce_2(u):
        landed(S1r.at[u], rR.at[1, u])
        for n in range(2):
            xn = m4(x + (1, 3)[n])
            total = UF[u, 2 * xn + c] + UR[u, xn].astype(F32)
            got = S1r[u, pl.ds(n * 128, 128), :].astype(F32)
            mine, plain = total[n * 128 : (n + 1) * 128], total[(1 - n) * 128 : (2 - n) * 128]
            S2s[u, n, pl.ds(n * 128, 128), :] = (mine + got).astype(BF16)
            S2s[u, n, pl.ds((1 - n) * 128, 128), :] = plain.astype(BF16)
            s2(u, n).start()

    def reduce_3(u):
        landed(S2r.at[u], rR.at[2, u])
        total = UF[u, q] + UR[u, x].astype(F32) + S2r[u, 0].astype(F32) + S2r[u, 1].astype(F32)
        out_user[u] = prior_a + TF[q, u].astype(F32) * total

    def blocks(ab, at):
        return (lambda h: IT[h, :, at, A, :]) if ab == 0 else (lambda h: IT[h, at, :, B, :])

    def along(ab, first):
        on_z = (ab == 0) == first
        return (z, lambda d: dev(dz=d)) if on_z else (y, lambda d: dev(dy=d))

    def j1(h, ab, n):
        _, to = along(ab, True)
        ref = pl.ds(2 * n, 2)
        return rc(J1s.at[h, ab, ref], J1r.at[h, ab, ref], send.at[7], jR.at[3, h], to((1, 3)[n]))

    def j2(h, ab, n):
        _, to = along(ab, True)
        return rc(J2s.at[h, ab, n], J2r.at[h, ab, n], send.at[8], jR.at[4, h], to((1, 3)[n]))

    def j3(h, ab, d):
        me, to = along(ab, False)
        return rc(
            J3s.at[h, ab, m4(me + d)], J3r.at[h, ab, d - 1], send.at[9], jR.at[5, h], to(d)
        )

    def item_1(h):
        for ab in range(2):
            me, _ = along(ab, True)
            J1s[h, ab] = blocks(ab, m4(me + 2))(h).astype(BF16)
            for n in range(2):
                j1(h, ab, n).start()

    def item_2(h):
        landed(J1r.at[h], jR.at[3, h])
        for ab in range(2):
            me, _ = along(ab, True)
            for n in range(2):
                part = blocks(ab, m4(me + (1, 3)[n]))(h)
                two, rest = slice(2 * n, 2 * n + 2), slice(2 - 2 * n, 4 - 2 * n)
                J2s[h, ab, n, two] = (part[two] + J1r[h, ab, two].astype(F32)).astype(BF16)
                J2s[h, ab, n, rest] = part[rest].astype(BF16)
                j2(h, ab, n).start()

    def item_3(h):
        landed(J2r.at[h], jR.at[4, h])
        for ab in range(2):
            me, _ = along(ab, True)
            total = blocks(ab, me)(h) + J2r[h, ab, 0].astype(F32) + J2r[h, ab, 1].astype(F32)
            J3s[h, ab] = total.astype(BF16)
            if ab == 0:
                IT[h, :, z, A, :] = total
            else:
                IT[h, y, :, B, :] = total
            for d in (1, 2, 3):
                j3(h, ab, d).start()

    def item_4(h):
        landed(J3r.at[h], jR.at[5, h])
        for ab in range(2):
            rows = (A, B)[ab]
            total = IT[h, y, z, rows, :] + jnp.sum(J3r[h, ab].astype(F32), axis=0)
            out_item[rows, h * 512 : (h + 1) * 512] = (
                prior_c + BT[h, y, z, rows, :].astype(F32) * total
            )

    def xi_send(n):
        dx, dc = item_peers[n]
        return rc(XIP, XR.at[q], send.at[13], tR.at[6], dev(dx=dx, dc=dc))

    def xi_1():
        XR[q] = XIP[...]
        for n in range(7):
            xi_send(n).start()

    def xi_2():
        landed(XR.at[pl.ds(0, 7)], tR.at[6])
        out_xi[...] = prior_a2 / prior_b2 + jnp.sum(XR[...], axis=0)

    def eta_z(d):
        return rc(EP0, ER1.at[z], send.at[14], tR.at[7], dev(dz=d))

    def eta_y(d):
        return rc(EP1, ER2.at[y], send.at[15], tR.at[8], dev(dy=d))

    def eta_1():
        for k8 in range(8):
            row = out_tot[1, k8 : k8 + 1, :]
            TTc[k8] = jnp.broadcast_to(row, (128, 128)).T
        for h in range(2):
            em = jnp.concatenate(
                [(prior_c2 + K * prior_c) / eta_ref[h * 4 + r : h * 4 + r + 1, :] for r in range(4)], axis=1
            )

            def step(k16, acc):
                yy, zz = k16 // 4, k16 % 4
                tt = TTc[k16 // 2, pl.ds(pl.multiple_of((k16 % 2) * 64, 64), 64), :]
                rate = jnp.concatenate([tt] * 4, axis=1) + em
                val = (prior_c / 16 + BT[h, yy, zz].astype(F32) * IT[h, yy, zz]) / rate
                return acc + jnp.sum(val.reshape(8, 8, 512), axis=0)

            acc = lax.fori_loop(0, 16, step, jnp.zeros((8, 512), F32))
            EP0[h] = jnp.sum(acc, axis=0, keepdims=True)
        ER1[z] = EP0[...]
        for d in (1, 2, 3):
            eta_z(d).start()

    def eta_2():
        landed(ER1.at[pl.ds(0, 3)], tR.at[7])
        EP1[...] = jnp.sum(ER1[...], axis=0)
        ER2[y] = EP1[...]
        for d in (1, 2, 3):
            eta_y(d).start()

    def eta_3():
        landed(ER2.at[pl.ds(0, 3)], tR.at[8])
        out_eta[...] = prior_c2 / prior_d2 + jnp.sum(ER2[...], axis=0)

    for d in be_loads:
        d.wait()
    sums = jnp.zeros((64, 128), F32)
    for ib in range(8):
        rows = slice(ib * 128, (ib + 1) * 128)
        e, mean = exp_mean_log(be_s_v[:, rows], be_r_v[:, rows])
        BT[ib // 4, y, z, :, (ib % 4) * 128 : (ib % 4 + 1) * 128] = e.astype(BF16)
        sums = sums + mean
    row = jnp.sum(jnp.concatenate([sums, sums], axis=0).T, axis=0, keepdims=True)
    lane = lax.broadcasted_iota(jnp.int32, (8, 128), 1)
    sub = lax.broadcasted_iota(jnp.int32, (8, 128), 0)
    TS0[0] = jnp.where((sub == p // 2) & (lane // 64 == p % 2), jnp.broadcast_to(row, (8, 128)), 0.0)
    TL[...] = jnp.zeros_like(TL)
    out_tot[...] = jnp.zeros_like(out_tot)
    th_loads[0].wait()
    th_loads[1].wait()
    pl.semaphore_wait(bar, 13)
    for h in range(2):
        for ab in range(2):
            for d in (1, 2, 3):
                b1(h, ab, d).start()

    def theta_total_1():
        local = jnp.sum(TL[...], axis=0, keepdims=True)
        TS0[1] = jnp.where(sub == q, jnp.broadcast_to(local, (8, 128)), 0.0)
        total_1(1)

    def clear():
        IT[...] = jnp.zeros_like(IT)
        counts_load.wait()

    def slot_step(s, carry):
        def at(slots, task):
            here = s == slots[0]
            block = jnp.int32(0)
            for t in slots[1:]:
                here = here | (s == t)
                block = block + (s >= t).astype(jnp.int32)

            @pl.when(here)
            def _():
                task(block)

        def once(slots, tasks):
            for t, task in zip(slots, tasks):
                pl.when(s == t)(task)

        def halves(slots, task):
            for h, t in enumerate(slots):
                pl.when(s == t)(lambda h=h: task(h))

        at(OWN, own)
        at(FORWARD_1, forward_1)
        at(FORWARD_2, forward_2)
        once([0, CLEAR], [lambda: total_1(0), clear])
        halves(BETA_2, beta_2)
        halves(BETA_3, beta_3)
        halves(BETA_4, beta_4)
        once(TOTAL_BETA, [lambda: total_2(0), lambda: total_3(0), lambda: total_4(0)])
        at(REDUCE_2, reduce_2)
        at(REDUCE_1, reduce_1)
        at(TILES, tiles)
        at(FIRST_HALF, lambda n: tiles_first(n + 4))
        at(SECOND_HALF, lambda n: tiles_second(n + 4))
        once(TOTAL_THETA, [theta_total_1, lambda: total_2(1), lambda: total_3(1), lambda: total_4(1)])
        halves(ITEM_1, item_1)
        halves(ITEM_2, item_2)
        once([XI[0], ETA[0]], [xi_1, eta_1])
        halves(ITEM_3, item_3)
        halves(ITEM_4, item_4)
        at(REDUCE_3, reduce_3)
        once([XI[1]] + ETA[1:], [xi_2, eta_2, eta_3])
        return carry

    lax.fori_loop(0, SLOTS, slot_step, 0)

    landed(BT.at[0, pl.ds(0, 3), :, A, :], send.at[0])
    landed(BT.at[0], send.at[1])
    landed(BT.at[0, pl.ds(0, 2)], send.at[2])
    landed(TF.at[pl.ds(0, 7)], send.at[3])
    landed(UR, send.at[4])
    landed(S1s, send.at[5])
    landed(S2s, send.at[6])
    landed(J1s, send.at[7])
    landed(J2s, send.at[8])
    landed(J3r, send.at[9])
    landed(TR1.at[:, pl.ds(0, 7)], send.at[10])
    landed(TR2.at[:, pl.ds(0, 3)], send.at[11])
    landed(TR3.at[:, pl.ds(0, 3)], send.at[12])
    landed(XR.at[pl.ds(0, 7)], send.at[13])
    landed(ER1.at[pl.ds(0, 3)], send.at[14])
    landed(ER2.at[pl.ds(0, 3)], send.at[15])


def write_out(
    user_new, item_new, xi_new, eta_new, totals, xi_ref, eta_ref, o_user, o_ulog, o_xi, o_item, o_ilog, o_eta, ulog, tt, sem
):
    user = lax.axis_index("user")
    item = lax.axis_index("item")
    copy_user = pltpu.make_async_copy(user_new, o_user, sem.at[0])
    copy_user.start()
    beta_total = totals[0, pl.ds(item, 1), :]
    for u in range(UB):
        for r in range(2):
            row = (prior_a2 + K * prior_a) / xi_ref[2 * u + r : 2 * u + r + 1, :]
            col = jnp.broadcast_to(row, (128, 128)).T
            ulog[u, r * 128 : (r + 1) * 128, :] = jnp.log(col + beta_total)
        pltpu.make_async_copy(ulog.at[u], o_ulog.at[u], sem.at[1]).start()
    tt[...] = jnp.broadcast_to(totals[1, pl.ds(user // 2, 1), :], (128, 128)).T
    theta_total = tt[pl.ds(pl.multiple_of((user % 2) * 64, 64), 64), :]
    for ib in range(8):
        row = (prior_c2 + K * prior_c) / eta_ref[ib : ib + 1, :]
        o_ilog[:, ib * 128 : (ib + 1) * 128] = jnp.log(theta_total + row)
    o_item[...] = item_new[...]
    o_xi[...] = xi_new[...]
    o_eta[...] = eta_new[...]
    copy_user.wait()
    pltpu.make_async_copy(ulog, o_ulog, sem.at[1]).wait()


def on_device(theta_shape, theta_rate, xi_rate, beta_shape, beta_rate, eta_rate, tile_slots, tile_counts, live_tiles):
    xi_rows, eta_rows = xi_rate.reshape(16, 128), eta_rate.reshape(8, 128)
    smem = pl.BlockSpec(memory_space=pltpu.SMEM)
    vmem = pl.BlockSpec(memory_space=pltpu.VMEM)
    hbm = pl.BlockSpec(memory_space=pltpu.HBM)
    dma = pltpu.SemaphoreType.DMA
    V = pltpu.VMEM
    user_new, item_new, xi_new, eta_new, totals = pl.pallas_call(
        kernel,
        out_shape=(
            V((8, 256, 128), F32),
            V((64, 1024), F32),
            V((8, 2, 128), F32),
            V((2, 1, 512), F32),
            V((2, 8, 128), F32),
        ),
        in_specs=[smem, smem, hbm, hbm, hbm, hbm, hbm, vmem, vmem],
        out_specs=(vmem,) * 5,
        scratch_shapes=[
            V((2048, 128), F32),
            V((2048, 128), F32),
            V((64, 1024), F32),
            V((64, 1024), F32),
            V((32, 256, 256), BF16),
            V((8, 8, 256, 128), BF16),
            V((2, 4, 4, 64, 512), BF16),
            V((2, 256, 512), BF16),
            V((2, 4, 4, 64, 512), F32),
            V((8, 8, 256, 128), F32),
            V((8, 4, 2, 256, 128), BF16),
            V((8, 4, 256, 128), BF16),
            V((8, 256, 128), BF16),
            V((8, 256, 128), BF16),
            V((8, 2, 256, 128), BF16),
            V((8, 2, 256, 128), BF16),
            V((2, 2, 4, 32, 512), BF16),
            V((2, 2, 4, 32, 512), BF16),
            V((2, 2, 2, 4, 32, 512), BF16),
            V((2, 2, 2, 4, 32, 512), BF16),
            V((2, 2, 4, 32, 512), BF16),
            V((2, 2, 3, 32, 512), BF16),
            V((8, 128), F32),
            V((2, 8, 128), F32),
            V((2, 8, 128), F32),
            V((2, 8, 128), F32),
            V((2, 8, 8, 128), F32),
            V((2, 4, 8, 128), F32),
            V((2, 4, 8, 128), F32),
            V((8, 128, 128), F32),
            V((8, 2, 128), F32),
            V((8, 8, 2, 128), F32),
            V((2, 1, 512), F32),
            V((2, 1, 512), F32),
            V((4, 2, 1, 512), F32),
            V((4, 2, 1, 512), F32),
                dma((4,)),
            dma((3, 8)),
            dma((3, 8)),
            dma((6, 2)),
            dma((9,)),
            dma((16,)),
        ],
        compiler_params=pltpu.CompilerParams(
            collective_id=0, has_side_effects=True, vmem_limit_bytes=58 * 2**20
        ),
        cost_estimate=pl.CostEstimate(flops=13 * 10**9, bytes_accessed=10 * 2**20, transcendentals=10**6),
        name="update",
    )(
        tile_slots.reshape(TMAX),
        live_tiles,
        theta_shape,
        theta_rate,
        beta_shape.T,
        beta_rate.T,
        tile_counts.reshape(TMAX, BLK, BLK),
        xi_rows,
        eta_rows,
    )
    out = jax.ShapeDtypeStruct
    o_user, o_ulog, o_xi, o_item, o_ilog, o_eta = pl.pallas_call(
        write_out,
        out_shape=(
            out((8, 256, 128), F32),
            out((8, 256, 128), F32),
            out((8, 2, 128), F32),
            out((64, 1024), F32),
            out((64, 1024), F32),
            out((2, 1, 512), F32),
        ),
        in_specs=[vmem] * 7,
        out_specs=(hbm, hbm, vmem, vmem, vmem, vmem),
        scratch_shapes=[V((8, 256, 128), F32), V((128, 128), F32), dma((2,))],
        compiler_params=pltpu.CompilerParams(vmem_limit_bytes=16 * 2**20),
        name="write_out",
    )(user_new, item_new, xi_new, eta_new, totals, xi_rows, eta_rows)
    return (
        o_user.reshape(2048, 128),
        o_ulog.reshape(2048, 128),
        o_xi.reshape(2048),
        o_item.T,
        o_ilog.T,
        o_eta.reshape(1024),
    )


def solution(mesh):
    in_specs = (
        P("user", "item"),
        P("user", "item"),
        P("user"),
        P("item", "user"),
        P("item", "user"),
        P("item"),
        P("user", "item", None),
        P("user", "item", None, None, None),
        P("user", "item"),
    )
    out_specs = (
        P("user", "item"),
        P("user", "item"),
        P("user"),
        P("item", "user"),
        P("item", "user"),
        P("item"),
    )
    return jax.shard_map(on_device, mesh=mesh, in_specs=in_specs, out_specs=out_specs, check_vma=False)
```

```python
import jax
import jax.numpy as jnp
from jax import lax
from jax.experimental import pallas as pl
from jax.experimental.pallas import tpu as pltpu
from jax.sharding import PartitionSpec as P

prior_a = 0.3
prior_a2 = 0.3
prior_b2 = 1.0
prior_c = 0.3
prior_c2 = 0.3
prior_d2 = 1.0

K = 1024
UB = 8
BLK = 256
TMAX = 32
F32 = jnp.float32
BF16 = jnp.bfloat16
MESH = pl.DeviceIdType.MESH
OWN = [0, 1, 2, 4, 5, 6, 7, 9]
FORWARD_1 = [4, 5, 6, 7, 9, 11, 12, 14]
FORWARD_2 = [7, 9, 11, 12, 14, 15, 16, 17]
TILES = [13, 14, 15, 16]
FIRST_HALF = [17, 19]
SECOND_HALF = [21, 22, 23, 24]
REDUCE_1 = [15, 16, 17, 19, 24, 25, 26, 27]
REDUCE_2 = [17, 19, 21, 22, 27, 28, 29, 30]
REDUCE_3 = [21, 23, 25, 26, 31, 32, 33, 34]
BETA_2 = [4, 5]
BETA_3 = [8, 10]
BETA_4 = [13, 13]
ITEM_1 = [19, 24]
ITEM_2 = [24, 28]
ITEM_3 = [30, 32]
ITEM_4 = [33, 35]
ETA = [26, 29, 31, 34]
XI = [25, 32]
TOTAL_BETA = [6, 8, 12]
TOTAL_THETA = [10, 14, 16, 19]
CLEAR = 3
SLOTS = 36


def exp_mean_log(s, r):
    w = s * (s + 3.0)
    prod = w * (w + 2.0)
    y = s + 4.0
    yr = y * r
    inv = 1.0 / (prod * yr)
    inv_prod = inv * yr
    v = inv * prod * r
    inv_r = inv * prod * y
    rec = (2.0 * s + 3.0) * (2.0 * w + 2.0) * inv_prod
    v2 = v * v
    series = v2 * (1.0 / 12 - v2 * (1.0 / 120 - v2 * (1.0 / 252 - v2 * (1.0 / 240))))
    return y * jnp.exp(-(rec + 0.5 * v + series)) * inv_r, s * inv_r


def kernel(
    slots_ref,
    live_ref,
    th_s,
    th_r,
    be_s,
    be_r,
    counts,
    xi_ref,
    eta_ref,
    out_user,
    out_item,
    out_xi,
    out_eta,
    out_tot,
    th_s_v,
    th_r_v,
    be_s_v,
    be_r_v,
    counts_v,
    TF,
    BT,
    R,
    IT,
    UF,
    U16,
    UR,
    S1s,
    S1r,
    S2s,
    S2r,
    J1s,
    J1r,
    J2s,
    J2r,
    J3s,
    J3r,
    TL,
    TS0,
    TS1,
    TS2,
    TR1,
    TR2,
    TR3,
    TTc,
    XIP,
    XR,
    EP0,
    EP1,
    ER1,
    ER2,
    lsem,
    gR,
    rR,
    jR,
    tR,
    send,
):
    user = lax.axis_index("user")
    item = lax.axis_index("item")
    x, c = item // 2, item % 2
    y, z = user // 4, user % 4
    q, p = item, user

    def m4(v):
        return (v + 4) % 4

    def dev(dx=0, dc=0, dy=0, dz=0):
        return (m4(y + dy) * 4 + m4(z + dz), m4(x + dx) * 2 + (c + dc) % 2)

    item_peers = [(dx, dc) for dx in range(4) for dc in range(2) if dx or dc]

    bar = pltpu.get_barrier_semaphore()
    for dx, dc in item_peers:
        pl.semaphore_signal(bar, inc=1, device_id=dev(dx=dx, dc=dc), device_id_type=MESH)
    for d in (1, 2, 3):
        pl.semaphore_signal(bar, inc=1, device_id=dev(dy=d), device_id_type=MESH)
        pl.semaphore_signal(bar, inc=1, device_id=dev(dz=d), device_id_type=MESH)

    be_loads = [
        pltpu.make_async_copy(be_s, be_s_v, lsem.at[0]),
        pltpu.make_async_copy(be_r, be_r_v, lsem.at[0]),
    ]
    first, later = pl.ds(0, BLK), pl.ds(BLK, 7 * BLK)
    th_loads = [
        pltpu.make_async_copy(th_s.at[first, :], th_s_v.at[first, :], lsem.at[1]),
        pltpu.make_async_copy(th_r.at[first, :], th_r_v.at[first, :], lsem.at[1]),
        pltpu.make_async_copy(th_s.at[later, :], th_s_v.at[later, :], lsem.at[2]),
        pltpu.make_async_copy(th_r.at[later, :], th_r_v.at[later, :], lsem.at[2]),
    ]
    counts_load = pltpu.make_async_copy(counts, counts_v, lsem.at[3])
    for d in be_loads + th_loads + [counts_load]:
        d.start()

    def landed(ref, sem):
        pltpu.make_async_copy(ref, ref, sem).wait()

    def rc(src, dst, ss, rs, to):
        return pltpu.make_async_remote_copy(
            src_ref=src, dst_ref=dst, send_sem=ss, recv_sem=rs, device_id=to, device_id_type=MESH
        )

    def total_item(k, n):
        dx, dc = item_peers[n]
        return rc(TS0.at[k], TR1.at[k, q], send.at[10], tR.at[3 * k], dev(dx=dx, dc=dc))

    def total_z(k, d):
        return rc(TS1.at[k], TR2.at[k, z], send.at[11], tR.at[3 * k + 1], dev(dz=d))

    def total_y(k, d):
        return rc(TS2.at[k], TR3.at[k, y], send.at[12], tR.at[3 * k + 2], dev(dy=d))

    def total_1(k):
        TR1[k, q] = TS0[k]
        for n in range(7):
            total_item(k, n).start()

    def total_2(k):
        landed(TR1.at[k, pl.ds(0, 7)], tR.at[3 * k])
        TS1[k] = jnp.sum(TR1[k], axis=0)
        TR2[k, z] = TS1[k]
        for d in (1, 2, 3):
            total_z(k, d).start()

    def total_3(k):
        landed(TR2.at[k, pl.ds(0, 3)], tR.at[3 * k + 1])
        TS2[k] = jnp.sum(TR2[k], axis=0)
        TR3[k, y] = TS2[k]
        for d in (1, 2, 3):
            total_y(k, d).start()

    def total_4(k):
        landed(TR3.at[k, pl.ds(0, 3)], tR.at[3 * k + 2])
        out_tot[k] = jnp.sum(TR3[k], axis=0)

    A, B = slice(0, 32), slice(32, 64)

    def b1(h, ab, d):
        rows = (A, B)[ab]
        ref = BT.at[h, y, z, rows, :]
        return rc(ref, ref, send.at[0], jR.at[0, h], dev(dy=d) if ab == 0 else dev(dz=d))

    def b2(h, ab, n):
        step = (1, 3)[n]
        if ab == 0:
            ref, to = BT.at[h, :, z, A, :], dev(dz=step)
        else:
            ref, to = BT.at[h, y, :, B, :], dev(dy=step)
        return rc(ref, ref, send.at[1], jR.at[1, h], to)

    def b3(h, ab, n):
        step, back = ((1, 3), (3, 1))[n]
        two = slice(0, 2) if n == 0 else slice(2, 4)
        if ab == 0:
            ref, to = BT.at[h, two, m4(z + back), A, :], dev(dz=step)
        else:
            ref, to = BT.at[h, m4(y + back), two, B, :], dev(dy=step)
        return rc(ref, ref, send.at[2], jR.at[2, h], to)

    def beta_2(h):
        landed(BT.at[h, pl.ds(0, 3), pl.ds(0, 2), A, :], jR.at[0, h])
        for ab in range(2):
            for n in range(2):
                b2(h, ab, n).start()

    def beta_3(h):
        landed(BT.at[h, pl.ds(0, 2)], jR.at[1, h])
        for ab in range(2):
            for n in range(2):
                b3(h, ab, n).start()

    def beta_4(h):
        landed(BT.at[h, 0], jR.at[2, h])

    def g(u, n):
        group = (0, 0, 2, 1, 1, 2, 2, 2)[n]
        q1, q3, q2 = m4(x + 1) * 2 + c, m4(x + 3) * 2 + c, m4(x + 2) * 2 + c
        ref, to = {
            0: (lambda: (TF.at[q, u], dev(dx=1))),
            1: (lambda: (TF.at[q, u], dev(dx=3))),
            2: (lambda: (TF.at[q, u], dev(dc=1))),
            3: (lambda: (TF.at[q3, u, pl.ds(0, 128), :], dev(dx=1))),
            4: (lambda: (TF.at[q1, u, pl.ds(128, 128), :], dev(dx=3))),
            5: (lambda: (TF.at[q3, u], dev(dc=1))),
            6: (lambda: (TF.at[q1, u], dev(dc=1))),
            7: (lambda: (TF.at[q2, u], dev(dc=1))),
        }[n]()
        return rc(ref, ref, send.at[3], gR.at[group, u], to)

    def own(u):
        @pl.when(u == 1)
        def _():
            th_loads[2].wait()
            th_loads[3].wait()

        rows = pl.ds(pl.multiple_of(u * BLK, BLK), BLK)
        e, mean = exp_mean_log(th_s_v[rows, :], th_r_v[rows, :])
        TF[q, u] = e.astype(BF16)
        TL[...] += jnp.sum(mean.reshape(32, 8, 128), axis=0)
        for n in (0, 1, 2):
            g(u, n).start()

    def forward_1(u):
        landed(TF.at[pl.ds(0, 2), u], gR.at[0, u])
        for n in (3, 5, 4, 6):
            g(u, n).start()

    def forward_2(u):
        landed(TF.at[0, u], gR.at[1, u])
        g(u, 7).start()

    def gathered(u):
        landed(TF.at[pl.ds(0, 4), u], gR.at[2, u])

    def factors(u, w):
        blocks = pl.ds(u, w)
        return [
            jnp.concatenate([TF[2 * kb + i, blocks].reshape(w * 256, 128) for i in range(2)], axis=1)
            for kb in range(4)
        ]

    def ratios(u, w, h, t_all):
        live = live_ref[0, 0]
        for n in range(2):
            cols = slice(n * 256, (n + 1) * 256)
            weights = BT[h, :, :, :, cols].reshape(K, 256)
            denominator = jnp.dot(t_all, weights, preferred_element_type=F32)
            for i in range(w):
                rows = slice(i * 256, (i + 1) * 256)
                pos = (u + i) * 4 + h * 2 + n
                slot = jnp.int32(0)
                for t in range(TMAX):
                    slot = jnp.where(slots_ref[t] == pos, t, slot)
                mask = (slot < live).astype(F32)
                tile_counts = counts_v[slot].astype(F32) * mask
                R[rows, h * 512 + n * 256 : h * 512 + (n + 1) * 256] = (tile_counts / denominator[rows]).astype(BF16)

    def user_terms(w, halves, kb):
        weights = jnp.concatenate([BT[h, kb].reshape(256, 512) for h in halves], axis=1)
        ratio = R[: w * 256, halves[0] * 512 : halves[-1] * 512 + 512]
        return lax.dot_general(ratio, weights, (((1,), (1,)), ((), ())), preferred_element_type=F32)

    def item_terms(w, t_blocks, halves):
        for kb in range(4):
            t_t = t_blocks[kb].T
            for h in halves:
                part = jnp.dot(t_t, R[: w * 256, h * 512 : (h + 1) * 512], preferred_element_type=F32)
                IT[h, kb] += part.reshape(4, 64, 512)

    def finish(u, t_blocks, product):
        x_col = []
        for r in range(2):
            row = (prior_a2 + K * prior_a) / xi_ref[pl.ds(2 * u + r, 1), :]
            x_col.append(jnp.broadcast_to(row, (128, 128)).T)
        xi_mean = jnp.concatenate(x_col, axis=0)
        acc = jnp.zeros((256, 128), F32)
        for kb in range(4):
            terms = product(kb)
            for half in range(2):
                k8, cols = 2 * kb + half, slice(half * 128, (half + 1) * 128)
                block = terms[:, cols]
                UF[u, k8] = block
                U16[u, k8 // 2, k8 % 2] = block.astype(BF16)
                rate = xi_mean + out_tot[0, k8 : k8 + 1, :]
                acc = acc + (prior_a / 8 + t_blocks[kb][:, cols].astype(F32) * block) / rate
        rows = [jnp.sum(acc[r * 128 : (r + 1) * 128].T, axis=0, keepdims=True) for r in range(2)]
        XIP[u] = jnp.concatenate(rows, axis=0)
        sib(u).start()

    def tiles(u):
        gathered(u)
        t_blocks = factors(u, 1)
        t_all = jnp.concatenate(t_blocks, axis=1)
        ratios(u, 1, 0, t_all)
        ratios(u, 1, 1, t_all)
        finish(u, t_blocks, lambda kb: user_terms(1, (0, 1), kb))
        item_terms(1, t_blocks, (0, 1))

    def tiles_first(n):
        u, w = 4 + 2 * n, 2
        for i in range(w):
            gathered(u + i)
        t_blocks = factors(u, w)
        ratios(u, w, 0, jnp.concatenate(t_blocks, axis=1))
        for kb in range(4):
            terms = user_terms(w, (0,), kb)
            for i in range(w):
                UF[u + i, 2 * kb] = terms[i * 256 : (i + 1) * 256, :128]
                UF[u + i, 2 * kb + 1] = terms[i * 256 : (i + 1) * 256, 128:]
        item_terms(w, t_blocks, (0,))

    def tiles_second(n):
        u = 4 + n
        t_blocks = factors(u, 1)
        ratios(u, 1, 1, jnp.concatenate(t_blocks, axis=1))

        def product(kb):
            before = jnp.concatenate([UF[u, 2 * kb], UF[u, 2 * kb + 1]], axis=1)
            return before + user_terms(1, (1,), kb)

        finish(u, t_blocks, product)
        item_terms(1, t_blocks, (1,))

    def sib(u):
        return rc(U16.at[u, :, 1 - c], UR.at[u], send.at[4], rR.at[0, u], dev(dc=1))

    def s1(u, n):
        rows = pl.ds(n * 128, 128)
        return rc(S1s.at[u, rows, :], S1r.at[u, rows, :], send.at[5], rR.at[1, u], dev(dx=(1, 3)[n]))

    def s2(u, n):
        return rc(S2s.at[u, n], S2r.at[u, n], send.at[6], rR.at[2, u], dev(dx=(1, 3)[n]))

    def reduce_1(u):
        landed(UR.at[u], rR.at[0, u])
        x2 = m4(x + 2)
        S1s[u] = (UF[u, 2 * x2 + c] + UR[u, x2].astype(F32)).astype(BF16)
        s1(u, 0).start()
        s1(u, 1).start()

    def reduce_2(u):
        landed(S1r.at[u], rR.at[1, u])
        for n in range(2):
            xn = m4(x + (1, 3)[n])
            total = UF[u, 2 * xn + c] + UR[u, xn].astype(F32)
            got = S1r[u, pl.ds(n * 128, 128), :].astype(F32)
            mine, plain = total[n * 128 : (n + 1) * 128], total[(1 - n) * 128 : (2 - n) * 128]
            S2s[u, n, pl.ds(n * 128, 128), :] = (mine + got).astype(BF16)
            S2s[u, n, pl.ds((1 - n) * 128, 128), :] = plain.astype(BF16)
            s2(u, n).start()

    def reduce_3(u):
        landed(S2r.at[u], rR.at[2, u])
        total = UF[u, q] + UR[u, x].astype(F32) + S2r[u, 0].astype(F32) + S2r[u, 1].astype(F32)
        out_user[u] = prior_a + TF[q, u].astype(F32) * total

    def blocks(ab, at):
        return (lambda h: IT[h, :, at, A, :]) if ab == 0 else (lambda h: IT[h, at, :, B, :])

    def along(ab, first):
        on_z = (ab == 0) == first
        return (z, lambda d: dev(dz=d)) if on_z else (y, lambda d: dev(dy=d))

    def j1(h, ab, n):
        _, to = along(ab, True)
        ref = pl.ds(2 * n, 2)
        return rc(J1s.at[h, ab, ref], J1r.at[h, ab, ref], send.at[7], jR.at[3, h], to((1, 3)[n]))

    def j2(h, ab, n):
        _, to = along(ab, True)
        return rc(J2s.at[h, ab, n], J2r.at[h, ab, n], send.at[8], jR.at[4, h], to((1, 3)[n]))

    def j3(h, ab, d):
        me, to = along(ab, False)
        return rc(
            J3s.at[h, ab, m4(me + d)], J3r.at[h, ab, d - 1], send.at[9], jR.at[5, h], to(d)
        )

    def item_1(h):
        for ab in range(2):
            me, _ = along(ab, True)
            J1s[h, ab] = blocks(ab, m4(me + 2))(h).astype(BF16)
            for n in range(2):
                j1(h, ab, n).start()

    def item_2(h):
        landed(J1r.at[h], jR.at[3, h])
        for ab in range(2):
            me, _ = along(ab, True)
            for n in range(2):
                part = blocks(ab, m4(me + (1, 3)[n]))(h)
                two, rest = slice(2 * n, 2 * n + 2), slice(2 - 2 * n, 4 - 2 * n)
                J2s[h, ab, n, two] = (part[two] + J1r[h, ab, two].astype(F32)).astype(BF16)
                J2s[h, ab, n, rest] = part[rest].astype(BF16)
                j2(h, ab, n).start()

    def item_3(h):
        landed(J2r.at[h], jR.at[4, h])
        for ab in range(2):
            me, _ = along(ab, True)
            total = blocks(ab, me)(h) + J2r[h, ab, 0].astype(F32) + J2r[h, ab, 1].astype(F32)
            J3s[h, ab] = total.astype(BF16)
            if ab == 0:
                IT[h, :, z, A, :] = total
            else:
                IT[h, y, :, B, :] = total
            for d in (1, 2, 3):
                j3(h, ab, d).start()

    def item_4(h):
        landed(J3r.at[h], jR.at[5, h])
        for ab in range(2):
            rows = (A, B)[ab]
            total = IT[h, y, z, rows, :] + jnp.sum(J3r[h, ab].astype(F32), axis=0)
            out_item[rows, h * 512 : (h + 1) * 512] = (
                prior_c + BT[h, y, z, rows, :].astype(F32) * total
            )

    def xi_send(n):
        dx, dc = item_peers[n]
        return rc(XIP, XR.at[q], send.at[13], tR.at[6], dev(dx=dx, dc=dc))

    def xi_1():
        XR[q] = XIP[...]
        for n in range(7):
            xi_send(n).start()

    def xi_2():
        landed(XR.at[pl.ds(0, 7)], tR.at[6])
        out_xi[...] = prior_a2 / prior_b2 + jnp.sum(XR[...], axis=0)

    def eta_z(d):
        return rc(EP0, ER1.at[z], send.at[14], tR.at[7], dev(dz=d))

    def eta_y(d):
        return rc(EP1, ER2.at[y], send.at[15], tR.at[8], dev(dy=d))

    def eta_1(h):
        if h == 0:
            for k8 in range(8):
                row = out_tot[1, k8 : k8 + 1, :]
                TTc[k8] = jnp.broadcast_to(row, (128, 128)).T
        em = jnp.concatenate(
            [(prior_c2 + K * prior_c) / eta_ref[h * 4 + r : h * 4 + r + 1, :] for r in range(4)], axis=1
        )

        def step(k16, acc):
            yy, zz = k16 // 4, k16 % 4
            tt = TTc[k16 // 2, pl.ds(pl.multiple_of((k16 % 2) * 64, 64), 64), :]
            rate = jnp.concatenate([tt] * 4, axis=1) + em
            val = (prior_c / 16 + BT[h, yy, zz].astype(F32) * IT[h, yy, zz]) / rate
            return acc + jnp.sum(val.reshape(8, 8, 512), axis=0)

        acc = lax.fori_loop(0, 16, step, jnp.zeros((8, 512), F32))
        EP0[h] = jnp.sum(acc, axis=0, keepdims=True)
        if h == 1:
            ER1[z] = EP0[...]
            for d in (1, 2, 3):
                eta_z(d).start()

    def eta_2():
        landed(ER1.at[pl.ds(0, 3)], tR.at[7])
        EP1[...] = jnp.sum(ER1[...], axis=0)
        ER2[y] = EP1[...]
        for d in (1, 2, 3):
            eta_y(d).start()

    def eta_3():
        landed(ER2.at[pl.ds(0, 3)], tR.at[8])
        out_eta[...] = prior_c2 / prior_d2 + jnp.sum(ER2[...], axis=0)

    for d in be_loads:
        d.wait()
    sums = jnp.zeros((64, 128), F32)
    for ib in range(8):
        rows = slice(ib * 128, (ib + 1) * 128)
        e, mean = exp_mean_log(be_s_v[:, rows], be_r_v[:, rows])
        BT[ib // 4, y, z, :, (ib % 4) * 128 : (ib % 4 + 1) * 128] = e.astype(BF16)
        sums = sums + mean
    row = jnp.sum(jnp.concatenate([sums, sums], axis=0).T, axis=0, keepdims=True)
    lane = lax.broadcasted_iota(jnp.int32, (8, 128), 1)
    sub = lax.broadcasted_iota(jnp.int32, (8, 128), 0)
    TS0[0] = jnp.where((sub == p // 2) & (lane // 64 == p % 2), jnp.broadcast_to(row, (8, 128)), 0.0)
    TL[...] = jnp.zeros_like(TL)
    out_tot[...] = jnp.zeros_like(out_tot)
    th_loads[0].wait()
    th_loads[1].wait()
    pl.semaphore_wait(bar, 13)
    for h in range(2):
        for ab in range(2):
            for d in (1, 2, 3):
                b1(h, ab, d).start()

    def theta_total_1():
        local = jnp.sum(TL[...], axis=0, keepdims=True)
        TS0[1] = jnp.where(sub == q, jnp.broadcast_to(local, (8, 128)), 0.0)
        total_1(1)

    def clear():
        IT[...] = jnp.zeros_like(IT)
        counts_load.wait()

    def slot_step(s, carry):
        def at(slots, task):
            here = s == slots[0]
            block = jnp.int32(0)
            for t in slots[1:]:
                here = here | (s == t)
                block = block + (s >= t).astype(jnp.int32)

            @pl.when(here)
            def _():
                task(block)

        def once(slots, tasks):
            for t, task in zip(slots, tasks):
                pl.when(s == t)(task)

        def halves(slots, task):
            for h, t in enumerate(slots):
                pl.when(s == t)(lambda h=h: task(h))

        at(FORWARD_2, forward_2)
        at(FORWARD_1, forward_1)
        at(OWN, own)
        once([0, CLEAR], [lambda: total_1(0), clear])
        halves(BETA_2, beta_2)
        halves(BETA_3, beta_3)
        halves(BETA_4, beta_4)
        once(TOTAL_BETA, [lambda: total_2(0), lambda: total_3(0), lambda: total_4(0)])
        at(REDUCE_2, reduce_2)
        at(REDUCE_1, reduce_1)
        at(TILES, tiles)
        at(FIRST_HALF, tiles_first)
        at(SECOND_HALF, tiles_second)
        once(TOTAL_THETA, [theta_total_1, lambda: total_2(1), lambda: total_3(1), lambda: total_4(1)])
        halves(ITEM_1, item_1)
        halves(ITEM_2, item_2)
        once([XI[0]], [xi_1])
        halves(ETA[:2], eta_1)
        halves(ITEM_3, item_3)
        halves(ITEM_4, item_4)
        at(REDUCE_3, reduce_3)
        once([XI[1]] + ETA[2:], [xi_2, eta_2, eta_3])
        return carry

    lax.fori_loop(0, SLOTS, slot_step, 0)

    landed(BT.at[0, pl.ds(0, 3), :, A, :], send.at[0])
    landed(BT.at[0], send.at[1])
    landed(BT.at[0, pl.ds(0, 2)], send.at[2])
    landed(TF.at[pl.ds(0, 7)], send.at[3])
    landed(UR, send.at[4])
    landed(S1s, send.at[5])
    landed(S2s, send.at[6])
    landed(J1s, send.at[7])
    landed(J2s, send.at[8])
    landed(J3r, send.at[9])
    landed(TR1.at[:, pl.ds(0, 7)], send.at[10])
    landed(TR2.at[:, pl.ds(0, 3)], send.at[11])
    landed(TR3.at[:, pl.ds(0, 3)], send.at[12])
    landed(XR.at[pl.ds(0, 7)], send.at[13])
    landed(ER1.at[pl.ds(0, 3)], send.at[14])
    landed(ER2.at[pl.ds(0, 3)], send.at[15])


def write_out(
    user_new, item_new, xi_new, eta_new, totals, xi_ref, eta_ref, o_user, o_ulog, o_xi, o_item, o_ilog, o_eta, ulog, tt, sem
):
    user = lax.axis_index("user")
    item = lax.axis_index("item")
    copy_user = pltpu.make_async_copy(user_new, o_user, sem.at[0])
    copy_user.start()
    beta_total = totals[0, pl.ds(item, 1), :]
    for u in range(UB):
        for r in range(2):
            row = (prior_a2 + K * prior_a) / xi_ref[2 * u + r : 2 * u + r + 1, :]
            col = jnp.broadcast_to(row, (128, 128)).T
            ulog[u, r * 128 : (r + 1) * 128, :] = jnp.log(col + beta_total)
        pltpu.make_async_copy(ulog.at[u], o_ulog.at[u], sem.at[1]).start()
    tt[...] = jnp.broadcast_to(totals[1, pl.ds(user // 2, 1), :], (128, 128)).T
    theta_total = tt[pl.ds(pl.multiple_of((user % 2) * 64, 64), 64), :]
    for ib in range(8):
        row = (prior_c2 + K * prior_c) / eta_ref[ib : ib + 1, :]
        o_ilog[:, ib * 128 : (ib + 1) * 128] = jnp.log(theta_total + row)
    o_item[...] = item_new[...]
    o_xi[...] = xi_new[...]
    o_eta[...] = eta_new[...]
    copy_user.wait()
    pltpu.make_async_copy(ulog, o_ulog, sem.at[1]).wait()


def on_device(theta_shape, theta_rate, xi_rate, beta_shape, beta_rate, eta_rate, tile_slots, tile_counts, live_tiles):
    xi_rows, eta_rows = xi_rate.reshape(16, 128), eta_rate.reshape(8, 128)
    smem = pl.BlockSpec(memory_space=pltpu.SMEM)
    vmem = pl.BlockSpec(memory_space=pltpu.VMEM)
    hbm = pl.BlockSpec(memory_space=pltpu.HBM)
    dma = pltpu.SemaphoreType.DMA
    V = pltpu.VMEM
    user_new, item_new, xi_new, eta_new, totals = pl.pallas_call(
        kernel,
        out_shape=(
            V((8, 256, 128), F32),
            V((64, 1024), F32),
            V((8, 2, 128), F32),
            V((2, 1, 512), F32),
            V((2, 8, 128), F32),
        ),
        in_specs=[smem, smem, hbm, hbm, hbm, hbm, hbm, vmem, vmem],
        out_specs=(vmem,) * 5,
        scratch_shapes=[
            V((2048, 128), F32),
            V((2048, 128), F32),
            V((64, 1024), F32),
            V((64, 1024), F32),
            V((32, 256, 256), BF16),
            V((8, 8, 256, 128), BF16),
            V((2, 4, 4, 64, 512), BF16),
            V((512, 1024), BF16),
            V((2, 4, 4, 64, 512), F32),
            V((8, 8, 256, 128), F32),
            V((8, 4, 2, 256, 128), BF16),
            V((8, 4, 256, 128), BF16),
            V((8, 256, 128), BF16),
            V((8, 256, 128), BF16),
            V((8, 2, 256, 128), BF16),
            V((8, 2, 256, 128), BF16),
            V((2, 2, 4, 32, 512), BF16),
            V((2, 2, 4, 32, 512), BF16),
            V((2, 2, 2, 4, 32, 512), BF16),
            V((2, 2, 2, 4, 32, 512), BF16),
            V((2, 2, 4, 32, 512), BF16),
            V((2, 2, 3, 32, 512), BF16),
            V((8, 128), F32),
            V((2, 8, 128), F32),
            V((2, 8, 128), F32),
            V((2, 8, 128), F32),
            V((2, 8, 8, 128), F32),
            V((2, 4, 8, 128), F32),
            V((2, 4, 8, 128), F32),
            V((8, 128, 128), F32),
            V((8, 2, 128), F32),
            V((8, 8, 2, 128), F32),
            V((2, 1, 512), F32),
            V((2, 1, 512), F32),
            V((4, 2, 1, 512), F32),
            V((4, 2, 1, 512), F32),
                dma((4,)),
            dma((3, 8)),
            dma((3, 8)),
            dma((6, 2)),
            dma((9,)),
            dma((16,)),
        ],
        compiler_params=pltpu.CompilerParams(
            collective_id=0, has_side_effects=True, vmem_limit_bytes=58 * 2**20
        ),
        cost_estimate=pl.CostEstimate(flops=13 * 10**9, bytes_accessed=10 * 2**20, transcendentals=10**6),
        name="update",
    )(
        tile_slots.reshape(TMAX),
        live_tiles,
        theta_shape,
        theta_rate,
        beta_shape.T,
        beta_rate.T,
        tile_counts.reshape(TMAX, BLK, BLK),
        xi_rows,
        eta_rows,
    )
    out = jax.ShapeDtypeStruct
    o_user, o_ulog, o_xi, o_item, o_ilog, o_eta = pl.pallas_call(
        write_out,
        out_shape=(
            out((8, 256, 128), F32),
            out((8, 256, 128), F32),
            out((8, 2, 128), F32),
            out((64, 1024), F32),
            out((64, 1024), F32),
            out((2, 1, 512), F32),
        ),
        in_specs=[vmem] * 7,
        out_specs=(hbm, hbm, vmem, vmem, vmem, vmem),
        scratch_shapes=[V((8, 256, 128), F32), V((128, 128), F32), dma((2,))],
        compiler_params=pltpu.CompilerParams(vmem_limit_bytes=16 * 2**20),
        name="write_out",
    )(user_new, item_new, xi_new, eta_new, totals, xi_rows, eta_rows)
    return (
        o_user.reshape(2048, 128),
        o_ulog.reshape(2048, 128),
        o_xi.reshape(2048),
        o_item.T,
        o_ilog.T,
        o_eta.reshape(1024),
    )


def solution(mesh):
    in_specs = (
        P("user", "item"),
        P("user", "item"),
        P("user"),
        P("item", "user"),
        P("item", "user"),
        P("item"),
        P("user", "item", None),
        P("user", "item", None, None, None),
        P("user", "item"),
    )
    out_specs = (
        P("user", "item"),
        P("user", "item"),
        P("user"),
        P("item", "user"),
        P("item", "user"),
        P("item"),
    )
    return jax.shard_map(on_device, mesh=mesh, in_specs=in_specs, out_specs=out_specs, check_vma=False)
```

```python
import jax
import jax.numpy as jnp
from jax import lax
from jax.experimental import pallas as pl
from jax.experimental.pallas import tpu as pltpu
from jax.sharding import PartitionSpec as P

prior_a = 0.3
prior_a2 = 0.3
prior_b2 = 1.0
prior_c = 0.3
prior_c2 = 0.3
prior_d2 = 1.0

K = 1024
UB = 8
BLK = 256
TMAX = 32
F32 = jnp.float32
BF16 = jnp.bfloat16
MESH = pl.DeviceIdType.MESH
OWN = [0, 1, 2, 4, 5, 6, 7, 9]
FORWARD_1 = [4, 5, 6, 7, 9, 11, 13, 14]
FORWARD_2 = [7, 9, 12, 13, 14, 15, 16, 17]
TILES = [15, 16]
FIRST_HALF = [12, 17, 19]
SECOND_HALF = [13, 14, 21, 22, 23, 24]
REDUCE_1 = [15, 16, 17, 19, 24, 25, 26, 27]
REDUCE_2 = [17, 19, 21, 22, 27, 28, 29, 30]
REDUCE_3 = [21, 23, 25, 26, 31, 32, 33, 34]
BETA_2 = [4, 5]
BETA_3 = [8, 10]
BETA_4 = [12, 13]
ITEM_1 = [19, 24]
ITEM_2 = [24, 27]
ITEM_3 = [29, 31]
ITEM_4 = [33, 35]
ETA = [26, 28, 31, 34]
XI = [25, 32]
TOTAL_BETA = [6, 8, 12]
TOTAL_THETA = [10, 14, 16, 19]
CLEAR = 3
SLOTS = 36


def exp_mean_log(s, r):
    w = s * (s + 3.0)
    prod = w * (w + 2.0)
    y = s + 4.0
    yr = y * r
    inv = 1.0 / (prod * yr)
    inv_prod = inv * yr
    v = inv * prod * r
    inv_r = inv * prod * y
    rec = (2.0 * s + 3.0) * (2.0 * w + 2.0) * inv_prod
    v2 = v * v
    series = v2 * (1.0 / 12 - v2 * (1.0 / 120 - v2 * (1.0 / 252 - v2 * (1.0 / 240))))
    return y * jnp.exp(-(rec + 0.5 * v + series)) * inv_r, s * inv_r


def kernel(
    slots_ref,
    live_ref,
    th_s,
    th_r,
    be_s,
    be_r,
    counts,
    xi_ref,
    eta_ref,
    out_user,
    out_item,
    out_xi,
    out_eta,
    out_tot,
    th_s_v,
    th_r_v,
    be_s_v,
    be_r_v,
    counts_v,
    TF,
    BT,
    R,
    IT,
    UF,
    U16,
    UR,
    S1s,
    S1r,
    S2s,
    S2r,
    J1s,
    J1r,
    J2s,
    J2r,
    J3s,
    J3r,
    TL,
    TS0,
    TS1,
    TS2,
    TR1,
    TR2,
    TR3,
    TTc,
    XIP,
    XR,
    EP0,
    EP1,
    ER1,
    ER2,
    lsem,
    gR,
    rR,
    jR,
    tR,
    send,
):
    user = lax.axis_index("user")
    item = lax.axis_index("item")
    x, c = item // 2, item % 2
    y, z = user // 4, user % 4
    q, p = item, user

    def m4(v):
        return (v + 4) % 4

    def dev(dx=0, dc=0, dy=0, dz=0):
        return (m4(y + dy) * 4 + m4(z + dz), m4(x + dx) * 2 + (c + dc) % 2)

    item_peers = [(dx, dc) for dx in range(4) for dc in range(2) if dx or dc]

    bar = pltpu.get_barrier_semaphore()
    for dx, dc in item_peers:
        pl.semaphore_signal(bar, inc=1, device_id=dev(dx=dx, dc=dc), device_id_type=MESH)
    for d in (1, 2, 3):
        pl.semaphore_signal(bar, inc=1, device_id=dev(dy=d), device_id_type=MESH)
        pl.semaphore_signal(bar, inc=1, device_id=dev(dz=d), device_id_type=MESH)

    be_loads = [
        pltpu.make_async_copy(be_s, be_s_v, lsem.at[0]),
        pltpu.make_async_copy(be_r, be_r_v, lsem.at[0]),
    ]
    first, later = pl.ds(0, BLK), pl.ds(BLK, 7 * BLK)
    th_loads = [
        pltpu.make_async_copy(th_s.at[first, :], th_s_v.at[first, :], lsem.at[1]),
        pltpu.make_async_copy(th_r.at[first, :], th_r_v.at[first, :], lsem.at[1]),
        pltpu.make_async_copy(th_s.at[later, :], th_s_v.at[later, :], lsem.at[2]),
        pltpu.make_async_copy(th_r.at[later, :], th_r_v.at[later, :], lsem.at[2]),
    ]
    counts_load = pltpu.make_async_copy(counts, counts_v, lsem.at[3])
    for d in be_loads + th_loads + [counts_load]:
        d.start()

    def landed(ref, sem):
        pltpu.make_async_copy(ref, ref, sem).wait()

    def rc(src, dst, ss, rs, to):
        return pltpu.make_async_remote_copy(
            src_ref=src, dst_ref=dst, send_sem=ss, recv_sem=rs, device_id=to, device_id_type=MESH
        )

    def total_item(k, n):
        dx, dc = item_peers[n]
        return rc(TS0.at[k], TR1.at[k, q], send.at[10], tR.at[3 * k], dev(dx=dx, dc=dc))

    def total_z(k, d):
        return rc(TS1.at[k], TR2.at[k, z], send.at[11], tR.at[3 * k + 1], dev(dz=d))

    def total_y(k, d):
        return rc(TS2.at[k], TR3.at[k, y], send.at[12], tR.at[3 * k + 2], dev(dy=d))

    def total_1(k):
        TR1[k, q] = TS0[k]
        for n in range(7):
            total_item(k, n).start()

    def total_2(k):
        landed(TR1.at[k, pl.ds(0, 7)], tR.at[3 * k])
        TS1[k] = jnp.sum(TR1[k], axis=0)
        TR2[k, z] = TS1[k]
        for d in (1, 2, 3):
            total_z(k, d).start()

    def total_3(k):
        landed(TR2.at[k, pl.ds(0, 3)], tR.at[3 * k + 1])
        TS2[k] = jnp.sum(TR2[k], axis=0)
        TR3[k, y] = TS2[k]
        for d in (1, 2, 3):
            total_y(k, d).start()

    def total_4(k):
        landed(TR3.at[k, pl.ds(0, 3)], tR.at[3 * k + 2])
        out_tot[k] = jnp.sum(TR3[k], axis=0)

    A, B = slice(0, 32), slice(32, 64)

    def b1(h, ab, d):
        rows = (A, B)[ab]
        ref = BT.at[h, y, z, rows, :]
        return rc(ref, ref, send.at[0], jR.at[0, h], dev(dy=d) if ab == 0 else dev(dz=d))

    def b2(h, ab, n):
        step = (1, 3)[n]
        if ab == 0:
            ref, to = BT.at[h, :, z, A, :], dev(dz=step)
        else:
            ref, to = BT.at[h, y, :, B, :], dev(dy=step)
        return rc(ref, ref, send.at[1], jR.at[1, h], to)

    def b3(h, ab, n):
        step, back = ((1, 3), (3, 1))[n]
        two = slice(0, 2) if n == 0 else slice(2, 4)
        if ab == 0:
            ref, to = BT.at[h, two, m4(z + back), A, :], dev(dz=step)
        else:
            ref, to = BT.at[h, m4(y + back), two, B, :], dev(dy=step)
        return rc(ref, ref, send.at[2], jR.at[2, h], to)

    def beta_2(h):
        landed(BT.at[h, pl.ds(0, 3), pl.ds(0, 2), A, :], jR.at[0, h])
        for ab in range(2):
            for n in range(2):
                b2(h, ab, n).start()

    def beta_3(h):
        landed(BT.at[h, pl.ds(0, 2)], jR.at[1, h])
        for ab in range(2):
            for n in range(2):
                b3(h, ab, n).start()

    def beta_4(h):
        landed(BT.at[h, 0], jR.at[2, h])

    def g(u, n):
        group = (0, 0, 2, 1, 1, 2, 2, 2)[n]
        q1, q3, q2 = m4(x + 1) * 2 + c, m4(x + 3) * 2 + c, m4(x + 2) * 2 + c
        ref, to = {
            0: (lambda: (TF.at[q, u], dev(dx=1))),
            1: (lambda: (TF.at[q, u], dev(dx=3))),
            2: (lambda: (TF.at[q, u], dev(dc=1))),
            3: (lambda: (TF.at[q3, u, pl.ds(0, 128), :], dev(dx=1))),
            4: (lambda: (TF.at[q1, u, pl.ds(128, 128), :], dev(dx=3))),
            5: (lambda: (TF.at[q3, u], dev(dc=1))),
            6: (lambda: (TF.at[q1, u], dev(dc=1))),
            7: (lambda: (TF.at[q2, u], dev(dc=1))),
        }[n]()
        return rc(ref, ref, send.at[3], gR.at[group, u], to)

    def own(u):
        @pl.when(u == 1)
        def _():
            th_loads[2].wait()
            th_loads[3].wait()

        rows = pl.ds(pl.multiple_of(u * BLK, BLK), BLK)
        e, mean = exp_mean_log(th_s_v[rows, :], th_r_v[rows, :])
        TF[q, u] = e.astype(BF16)
        TL[...] += jnp.sum(mean.reshape(32, 8, 128), axis=0)
        for n in (0, 1, 2):
            g(u, n).start()

    def forward_1(u):
        landed(TF.at[pl.ds(0, 2), u], gR.at[0, u])
        for n in (3, 5, 4, 6):
            g(u, n).start()

    def forward_2(u):
        landed(TF.at[0, u], gR.at[1, u])
        g(u, 7).start()

    def gathered(u):
        landed(TF.at[pl.ds(0, 4), u], gR.at[2, u])

    def factors(u, w):
        blocks = pl.ds(u, w)
        return [
            jnp.concatenate([TF[2 * kb + i, blocks].reshape(w * 256, 128) for i in range(2)], axis=1)
            for kb in range(4)
        ]

    def ratios(u, w, h, t_all):
        live = live_ref[0, 0]
        for n in range(2):
            cols = slice(n * 256, (n + 1) * 256)
            weights = BT[h, :, :, :, cols].reshape(K, 256)
            denominator = jnp.dot(t_all, weights, preferred_element_type=F32)
            for i in range(w):
                rows = slice(i * 256, (i + 1) * 256)
                pos = (u + i) * 4 + h * 2 + n
                slot = jnp.int32(0)
                for t in range(TMAX):
                    slot = jnp.where(slots_ref[t] == pos, t, slot)
                mask = (slot < live).astype(F32)
                tile_counts = counts_v[slot].astype(F32) * mask
                R[rows, h * 512 + n * 256 : h * 512 + (n + 1) * 256] = (tile_counts / denominator[rows]).astype(BF16)

    def user_terms(w, halves, kb):
        weights = jnp.concatenate([BT[h, kb].reshape(256, 512) for h in halves], axis=1)
        ratio = R[: w * 256, halves[0] * 512 : halves[-1] * 512 + 512]
        return lax.dot_general(ratio, weights, (((1,), (1,)), ((), ())), preferred_element_type=F32)

    def item_terms(w, t_blocks, halves):
        for kb in range(4):
            t_t = t_blocks[kb].T
            for h in halves:
                part = jnp.dot(t_t, R[: w * 256, h * 512 : (h + 1) * 512], preferred_element_type=F32)
                IT[h, kb] += part.reshape(4, 64, 512)

    def finish(u, t_blocks, product):
        x_col = []
        for r in range(2):
            row = (prior_a2 + K * prior_a) / xi_ref[pl.ds(2 * u + r, 1), :]
            x_col.append(jnp.broadcast_to(row, (128, 128)).T)
        xi_mean = jnp.concatenate(x_col, axis=0)
        acc = jnp.zeros((256, 128), F32)
        for kb in range(4):
            terms = product(kb)
            for half in range(2):
                k8, cols = 2 * kb + half, slice(half * 128, (half + 1) * 128)
                block = terms[:, cols]
                UF[u, k8] = block
                U16[u, k8 // 2, k8 % 2] = block.astype(BF16)
                rate = xi_mean + out_tot[0, k8 : k8 + 1, :]
                acc = acc + (prior_a / 8 + t_blocks[kb][:, cols].astype(F32) * block) / rate
        rows = [jnp.sum(acc[r * 128 : (r + 1) * 128].T, axis=0, keepdims=True) for r in range(2)]
        XIP[u] = jnp.concatenate(rows, axis=0)
        sib(u).start()

    def tiles(n):
        u = n + 2
        gathered(u)
        t_blocks = factors(u, 1)
        t_all = jnp.concatenate(t_blocks, axis=1)
        ratios(u, 1, 0, t_all)
        ratios(u, 1, 1, t_all)
        finish(u, t_blocks, lambda kb: user_terms(1, (0, 1), kb))
        item_terms(1, t_blocks, (0, 1))

    def tiles_first(n):
        u, w = 2 * n + 2 * (n >= 1).astype(jnp.int32), 2
        for i in range(w):
            gathered(u + i)
        t_blocks = factors(u, w)
        ratios(u, w, 0, jnp.concatenate(t_blocks, axis=1))
        for kb in range(4):
            terms = user_terms(w, (0,), kb)
            for i in range(w):
                UF[u + i, 2 * kb] = terms[i * 256 : (i + 1) * 256, :128]
                UF[u + i, 2 * kb + 1] = terms[i * 256 : (i + 1) * 256, 128:]
        item_terms(w, t_blocks, (0,))

    def tiles_second(n):
        u = n + 2 * (n >= 2).astype(jnp.int32)
        t_blocks = factors(u, 1)
        ratios(u, 1, 1, jnp.concatenate(t_blocks, axis=1))

        def product(kb):
            before = jnp.concatenate([UF[u, 2 * kb], UF[u, 2 * kb + 1]], axis=1)
            return before + user_terms(1, (1,), kb)

        finish(u, t_blocks, product)
        item_terms(1, t_blocks, (1,))

    def sib(u):
        return rc(U16.at[u, :, 1 - c], UR.at[u], send.at[4], rR.at[0, u], dev(dc=1))

    def s1(u, n):
        rows = pl.ds(n * 128, 128)
        return rc(S1s.at[u, rows, :], S1r.at[u, rows, :], send.at[5], rR.at[1, u], dev(dx=(1, 3)[n]))

    def s2(u, n):
        return rc(S2s.at[u, n], S2r.at[u, n], send.at[6], rR.at[2, u], dev(dx=(1, 3)[n]))

    def reduce_1(u):
        landed(UR.at[u], rR.at[0, u])
        x2 = m4(x + 2)
        S1s[u] = (UF[u, 2 * x2 + c] + UR[u, x2].astype(F32)).astype(BF16)
        s1(u, 0).start()
        s1(u, 1).start()

    def reduce_2(u):
        landed(S1r.at[u], rR.at[1, u])
        for n in range(2):
            xn = m4(x + (1, 3)[n])
            total = UF[u, 2 * xn + c] + UR[u, xn].astype(F32)
            got = S1r[u, pl.ds(n * 128, 128), :].astype(F32)
            mine, plain = total[n * 128 : (n + 1) * 128], total[(1 - n) * 128 : (2 - n) * 128]
            S2s[u, n, pl.ds(n * 128, 128), :] = (mine + got).astype(BF16)
            S2s[u, n, pl.ds((1 - n) * 128, 128), :] = plain.astype(BF16)
            s2(u, n).start()

    def reduce_3(u):
        landed(S2r.at[u], rR.at[2, u])
        total = UF[u, q] + UR[u, x].astype(F32) + S2r[u, 0].astype(F32) + S2r[u, 1].astype(F32)
        out_user[u] = prior_a + TF[q, u].astype(F32) * total

    def blocks(ab, at):
        return (lambda h: IT[h, :, at, A, :]) if ab == 0 else (lambda h: IT[h, at, :, B, :])

    def along(ab, first):
        on_z = (ab == 0) == first
        return (z, lambda d: dev(dz=d)) if on_z else (y, lambda d: dev(dy=d))

    def j1(h, ab, n):
        _, to = along(ab, True)
        ref = pl.ds(2 * n, 2)
        return rc(J1s.at[h, ab, ref], J1r.at[h, ab, ref], send.at[7], jR.at[3, h], to((1, 3)[n]))

    def j2(h, ab, n):
        _, to = along(ab, True)
        return rc(J2s.at[h, ab, n], J2r.at[h, ab, n], send.at[8], jR.at[4, h], to((1, 3)[n]))

    def j3(h, ab, d):
        me, to = along(ab, False)
        return rc(
            J3s.at[h, ab, m4(me + d)], J3r.at[h, ab, d - 1], send.at[9], jR.at[5, h], to(d)
        )

    def item_1(h):
        for ab in range(2):
            me, _ = along(ab, True)
            J1s[h, ab] = blocks(ab, m4(me + 2))(h).astype(BF16)
            for n in range(2):
                j1(h, ab, n).start()

    def item_2(h):
        landed(J1r.at[h], jR.at[3, h])
        for ab in range(2):
            me, _ = along(ab, True)
            for n in range(2):
                part = blocks(ab, m4(me + (1, 3)[n]))(h)
                two, rest = slice(2 * n, 2 * n + 2), slice(2 - 2 * n, 4 - 2 * n)
                J2s[h, ab, n, two] = (part[two] + J1r[h, ab, two].astype(F32)).astype(BF16)
                J2s[h, ab, n, rest] = part[rest].astype(BF16)
                j2(h, ab, n).start()

    def item_3(h):
        landed(J2r.at[h], jR.at[4, h])
        for ab in range(2):
            me, _ = along(ab, True)
            total = blocks(ab, me)(h) + J2r[h, ab, 0].astype(F32) + J2r[h, ab, 1].astype(F32)
            J3s[h, ab] = total.astype(BF16)
            if ab == 0:
                IT[h, :, z, A, :] = total
            else:
                IT[h, y, :, B, :] = total
            for d in (1, 2, 3):
                j3(h, ab, d).start()

    def item_4(h):
        landed(J3r.at[h], jR.at[5, h])
        for ab in range(2):
            rows = (A, B)[ab]
            total = IT[h, y, z, rows, :] + jnp.sum(J3r[h, ab].astype(F32), axis=0)
            out_item[rows, h * 512 : (h + 1) * 512] = (
                prior_c + BT[h, y, z, rows, :].astype(F32) * total
            )

    def xi_send(n):
        dx, dc = item_peers[n]
        return rc(XIP, XR.at[q], send.at[13], tR.at[6], dev(dx=dx, dc=dc))

    def xi_1():
        XR[q] = XIP[...]
        for n in range(7):
            xi_send(n).start()

    def xi_2():
        landed(XR.at[pl.ds(0, 7)], tR.at[6])
        out_xi[...] = prior_a2 / prior_b2 + jnp.sum(XR[...], axis=0)

    def eta_z(d):
        return rc(EP0, ER1.at[z], send.at[14], tR.at[7], dev(dz=d))

    def eta_y(d):
        return rc(EP1, ER2.at[y], send.at[15], tR.at[8], dev(dy=d))

    def eta_1(h):
        if h == 0:
            for k8 in range(8):
                row = out_tot[1, k8 : k8 + 1, :]
                TTc[k8] = jnp.broadcast_to(row, (128, 128)).T
        em = jnp.concatenate(
            [(prior_c2 + K * prior_c) / eta_ref[h * 4 + r : h * 4 + r + 1, :] for r in range(4)], axis=1
        )

        def step(k16, acc):
            yy, zz = k16 // 4, k16 % 4
            tt = TTc[k16 // 2, pl.ds(pl.multiple_of((k16 % 2) * 64, 64), 64), :]
            rate = jnp.concatenate([tt] * 4, axis=1) + em
            val = (prior_c / 16 + BT[h, yy, zz].astype(F32) * IT[h, yy, zz]) / rate
            return acc + jnp.sum(val.reshape(8, 8, 512), axis=0)

        acc = lax.fori_loop(0, 16, step, jnp.zeros((8, 512), F32))
        EP0[h] = jnp.sum(acc, axis=0, keepdims=True)
        if h == 1:
            ER1[z] = EP0[...]
            for d in (1, 2, 3):
                eta_z(d).start()

    def eta_2():
        landed(ER1.at[pl.ds(0, 3)], tR.at[7])
        EP1[...] = jnp.sum(ER1[...], axis=0)
        ER2[y] = EP1[...]
        for d in (1, 2, 3):
            eta_y(d).start()

    def eta_3():
        landed(ER2.at[pl.ds(0, 3)], tR.at[8])
        out_eta[...] = prior_c2 / prior_d2 + jnp.sum(ER2[...], axis=0)

    for d in be_loads:
        d.wait()
    sums = jnp.zeros((64, 128), F32)
    for ib in range(8):
        rows = slice(ib * 128, (ib + 1) * 128)
        e, mean = exp_mean_log(be_s_v[:, rows], be_r_v[:, rows])
        BT[ib // 4, y, z, :, (ib % 4) * 128 : (ib % 4 + 1) * 128] = e.astype(BF16)
        sums = sums + mean
    row = jnp.sum(jnp.concatenate([sums, sums], axis=0).T, axis=0, keepdims=True)
    lane = lax.broadcasted_iota(jnp.int32, (8, 128), 1)
    sub = lax.broadcasted_iota(jnp.int32, (8, 128), 0)
    TS0[0] = jnp.where((sub == p // 2) & (lane // 64 == p % 2), jnp.broadcast_to(row, (8, 128)), 0.0)
    TL[...] = jnp.zeros_like(TL)
    out_tot[...] = jnp.zeros_like(out_tot)
    th_loads[0].wait()
    th_loads[1].wait()
    pl.semaphore_wait(bar, 13)
    for h in range(2):
        for ab in range(2):
            for d in (1, 2, 3):
                b1(h, ab, d).start()

    def theta_total_1():
        local = jnp.sum(TL[...], axis=0, keepdims=True)
        TS0[1] = jnp.where(sub == q, jnp.broadcast_to(local, (8, 128)), 0.0)
        total_1(1)

    def clear():
        IT[...] = jnp.zeros_like(IT)
        counts_load.wait()

    def slot_step(s, carry):
        def at(slots, task):
            here = s == slots[0]
            block = jnp.int32(0)
            for t in slots[1:]:
                here = here | (s == t)
                block = block + (s >= t).astype(jnp.int32)

            @pl.when(here)
            def _():
                task(block)

        def once(slots, tasks):
            for t, task in zip(slots, tasks):
                pl.when(s == t)(task)

        def halves(slots, task):
            for h, t in enumerate(slots):
                pl.when(s == t)(lambda h=h: task(h))

        at(FORWARD_2, forward_2)
        at(FORWARD_1, forward_1)
        at(OWN, own)
        once([0, CLEAR], [lambda: total_1(0), clear])
        halves(BETA_2, beta_2)
        halves(BETA_3, beta_3)
        halves(BETA_4, beta_4)
        once(TOTAL_BETA, [lambda: total_2(0), lambda: total_3(0), lambda: total_4(0)])
        at(REDUCE_2, reduce_2)
        at(REDUCE_1, reduce_1)
        at(TILES, tiles)
        at(FIRST_HALF, tiles_first)
        at(SECOND_HALF, tiles_second)
        once(TOTAL_THETA, [theta_total_1, lambda: total_2(1), lambda: total_3(1), lambda: total_4(1)])
        halves(ITEM_1, item_1)
        halves(ITEM_2, item_2)
        once([XI[0]], [xi_1])
        halves(ETA[:2], eta_1)
        halves(ITEM_3, item_3)
        halves(ITEM_4, item_4)
        at(REDUCE_3, reduce_3)
        once([XI[1]] + ETA[2:], [xi_2, eta_2, eta_3])
        return carry

    lax.fori_loop(0, SLOTS, slot_step, 0)

    landed(BT.at[0, pl.ds(0, 3), :, A, :], send.at[0])
    landed(BT.at[0], send.at[1])
    landed(BT.at[0, pl.ds(0, 2)], send.at[2])
    landed(TF.at[pl.ds(0, 7)], send.at[3])
    landed(UR, send.at[4])
    landed(S1s, send.at[5])
    landed(S2s, send.at[6])
    landed(J1s, send.at[7])
    landed(J2s, send.at[8])
    landed(J3r, send.at[9])
    landed(TR1.at[:, pl.ds(0, 7)], send.at[10])
    landed(TR2.at[:, pl.ds(0, 3)], send.at[11])
    landed(TR3.at[:, pl.ds(0, 3)], send.at[12])
    landed(XR.at[pl.ds(0, 7)], send.at[13])
    landed(ER1.at[pl.ds(0, 3)], send.at[14])
    landed(ER2.at[pl.ds(0, 3)], send.at[15])


def write_out(
    user_new, item_new, xi_new, eta_new, totals, xi_ref, eta_ref, o_user, o_ulog, o_xi, o_item, o_ilog, o_eta, ulog, tt, sem
):
    user = lax.axis_index("user")
    item = lax.axis_index("item")
    copy_user = pltpu.make_async_copy(user_new, o_user, sem.at[0])
    copy_user.start()
    beta_total = totals[0, pl.ds(item, 1), :]
    for u in range(UB):
        for r in range(2):
            row = (prior_a2 + K * prior_a) / xi_ref[2 * u + r : 2 * u + r + 1, :]
            col = jnp.broadcast_to(row, (128, 128)).T
            ulog[u, r * 128 : (r + 1) * 128, :] = jnp.log(col + beta_total)
        pltpu.make_async_copy(ulog.at[u], o_ulog.at[u], sem.at[1]).start()
    tt[...] = jnp.broadcast_to(totals[1, pl.ds(user // 2, 1), :], (128, 128)).T
    theta_total = tt[pl.ds(pl.multiple_of((user % 2) * 64, 64), 64), :]
    for ib in range(8):
        row = (prior_c2 + K * prior_c) / eta_ref[ib : ib + 1, :]
        o_ilog[:, ib * 128 : (ib + 1) * 128] = jnp.log(theta_total + row)
    o_item[...] = item_new[...]
    o_xi[...] = xi_new[...]
    o_eta[...] = eta_new[...]
    copy_user.wait()
    pltpu.make_async_copy(ulog, o_ulog, sem.at[1]).wait()


def on_device(theta_shape, theta_rate, xi_rate, beta_shape, beta_rate, eta_rate, tile_slots, tile_counts, live_tiles):
    xi_rows, eta_rows = xi_rate.reshape(16, 128), eta_rate.reshape(8, 128)
    smem = pl.BlockSpec(memory_space=pltpu.SMEM)
    vmem = pl.BlockSpec(memory_space=pltpu.VMEM)
    hbm = pl.BlockSpec(memory_space=pltpu.HBM)
    dma = pltpu.SemaphoreType.DMA
    V = pltpu.VMEM
    user_new, item_new, xi_new, eta_new, totals = pl.pallas_call(
        kernel,
        out_shape=(
            V((8, 256, 128), F32),
            V((64, 1024), F32),
            V((8, 2, 128), F32),
            V((2, 1, 512), F32),
            V((2, 8, 128), F32),
        ),
        in_specs=[smem, smem, hbm, hbm, hbm, hbm, hbm, vmem, vmem],
        out_specs=(vmem,) * 5,
        scratch_shapes=[
            V((2048, 128), F32),
            V((2048, 128), F32),
            V((64, 1024), F32),
            V((64, 1024), F32),
            V((32, 256, 256), BF16),
            V((8, 8, 256, 128), BF16),
            V((2, 4, 4, 64, 512), BF16),
            V((512, 1024), BF16),
            V((2, 4, 4, 64, 512), F32),
            V((8, 8, 256, 128), F32),
            V((8, 4, 2, 256, 128), BF16),
            V((8, 4, 256, 128), BF16),
            V((8, 256, 128), BF16),
            V((8, 256, 128), BF16),
            V((8, 2, 256, 128), BF16),
            V((8, 2, 256, 128), BF16),
            V((2, 2, 4, 32, 512), BF16),
            V((2, 2, 4, 32, 512), BF16),
            V((2, 2, 2, 4, 32, 512), BF16),
            V((2, 2, 2, 4, 32, 512), BF16),
            V((2, 2, 4, 32, 512), BF16),
            V((2, 2, 3, 32, 512), BF16),
            V((8, 128), F32),
            V((2, 8, 128), F32),
            V((2, 8, 128), F32),
            V((2, 8, 128), F32),
            V((2, 8, 8, 128), F32),
            V((2, 4, 8, 128), F32),
            V((2, 4, 8, 128), F32),
            V((8, 128, 128), F32),
            V((8, 2, 128), F32),
            V((8, 8, 2, 128), F32),
            V((2, 1, 512), F32),
            V((2, 1, 512), F32),
            V((4, 2, 1, 512), F32),
            V((4, 2, 1, 512), F32),
                dma((4,)),
            dma((3, 8)),
            dma((3, 8)),
            dma((6, 2)),
            dma((9,)),
            dma((16,)),
        ],
        compiler_params=pltpu.CompilerParams(
            collective_id=0, has_side_effects=True, vmem_limit_bytes=58 * 2**20
        ),
        cost_estimate=pl.CostEstimate(flops=13 * 10**9, bytes_accessed=10 * 2**20, transcendentals=10**6),
        name="update",
    )(
        tile_slots.reshape(TMAX),
        live_tiles,
        theta_shape,
        theta_rate,
        beta_shape.T,
        beta_rate.T,
        tile_counts.reshape(TMAX, BLK, BLK),
        xi_rows,
        eta_rows,
    )
    out = jax.ShapeDtypeStruct
    o_user, o_ulog, o_xi, o_item, o_ilog, o_eta = pl.pallas_call(
        write_out,
        out_shape=(
            out((8, 256, 128), F32),
            out((8, 256, 128), F32),
            out((8, 2, 128), F32),
            out((64, 1024), F32),
            out((64, 1024), F32),
            out((2, 1, 512), F32),
        ),
        in_specs=[vmem] * 7,
        out_specs=(hbm, hbm, vmem, vmem, vmem, vmem),
        scratch_shapes=[V((8, 256, 128), F32), V((128, 128), F32), dma((2,))],
        compiler_params=pltpu.CompilerParams(vmem_limit_bytes=16 * 2**20),
        name="write_out",
    )(user_new, item_new, xi_new, eta_new, totals, xi_rows, eta_rows)
    return (
        o_user.reshape(2048, 128),
        o_ulog.reshape(2048, 128),
        o_xi.reshape(2048),
        o_item.T,
        o_ilog.T,
        o_eta.reshape(1024),
    )


def solution(mesh):
    in_specs = (
        P("user", "item"),
        P("user", "item"),
        P("user"),
        P("item", "user"),
        P("item", "user"),
        P("item"),
        P("user", "item", None),
        P("user", "item", None, None, None),
        P("user", "item"),
    )
    out_specs = (
        P("user", "item"),
        P("user", "item"),
        P("user"),
        P("item", "user"),
        P("item", "user"),
        P("item"),
    )
    return jax.shard_map(on_device, mesh=mesh, in_specs=in_specs, out_specs=out_specs, check_vma=False)
```
